32 devices in a mesh: req: 8 (over y, x, core), tp: 4 (over z).
Axes of the slice: x: 2, y: 2, z: 4, core: 2. Of those that a mesh axis runs over, the one named last changes fastest.
Arguments:
- hidden_in: bfloat16 [2048, 2304], P('req'), may hold values from -6 to 6
- cache_lengths: int32 [8], P('req'), may hold values from 128 to 2048, as said below
- key_cache: bfloat16 [8, 2048, 2304], P('req', None, 'tp'), may hold values from -104 to 104
- value_cache: bfloat16 [8, 2048, 2304], P('req', None, 'tp'), may hold values from -6 to 6
- attn_norm: float32 [2304], replicated, may hold values from 0.5 to 1.5
- w_qkv: bfloat16 [3, 2304, 2304], P(None, None, 'tp'), may hold values from -0.125 to 0.125
- w_out: bfloat16 [2304, 2304], P('tp'), may hold values from -0.125 to 0.125
- ffn_norm: float32 [2304], replicated, may hold values from 0.5 to 1.5
- router: bfloat16 [2304, 8], replicated, may hold values from -0.125 to 0.125
- routes: int32 [2048, 2], P('req'), may hold values from 0 to 7, all different within a row; in each aligned block of 256 rows (0 to 255, 256 to 511, ...) at most 96 rows name the same one
- expert_gate: bfloat16 [8, 2304, 5760], P('req', None, 'tp'), may hold values from -0.125 to 0.125
- expert_up: bfloat16 [8, 2304, 5760], P('req', None, 'tp'), may hold values from -0.125 to 0.125
- expert_down: bfloat16 [8, 5760, 2304], P('req', 'tp'), may hold values from -0.078125 to 0.078125
Outputs:
- block_out: bfloat16 [2048, 2304], P(('req', 'tp'))
The draws below stay inside these ranges and needn't reach their ends.
Inputs may be any that keep to these rules, and one draw needn't show every extreme that they name: `cache_lengths`: some request has exactly 2048 cached tokens. `routes`: within the 256 rows of one request no expert is named by more than 96 rows, and in every draw, within some request, an expert is named by exactly 96 rows; a row's two experts differ.
All inputs are finite; a program needn't handle non-finite values.
Results may differ from the reference program's by a relative error of at most 0.013.
Values may be sent and summed in bfloat16 or wider, within the bound.
No kernel may reach another device: no remote copies, remote signals or barrier semaphores. Data moves between devices by JAX's collectives and lax.ppermute only.
A program may use at most 192 MiB of HBM per device.

```python
import math
import jax
import jax.numpy as jnp
import numpy as np
from jax import lax

D = 2304
HEAD = 64
FF = 5760
EXPERTS = 8
TOP = 2
TOK = 256
CACHE = 2048
HD = 2304
REQUESTS = 8
TOKENS = 2048
SUB = 1
CAP = 96
N_REQ = 8
N_TP = 4


def draw_cache_lengths(key, part):
    first_key, second_key = jax.random.split(key)
    spread = jax.random.randint(first_key, (REQUESTS,), 0, CACHE + 1)
    lengths = jnp.maximum(CACHE // 16, spread * spread // CACHE)
    chosen = jax.random.randint(second_key, (), 0, REQUESTS)
    return lengths.at[chosen].set(CACHE).astype(jnp.int32)


def draw_key_cache(key, part):
    first_key = jax.random.fold_in(key, 0)
    result = jax.random.truncated_normal(first_key, -6.0, 6.0, (REQUESTS, CACHE, HD), jnp.float32)
    return result.astype(jnp.bfloat16)


def levels(stream_key, shape, cuts, low, largest):
    factor_of = 1.0
    for dim, blocks in cuts:
        heights = jax.random.uniform(jax.random.fold_in(jax.random.fold_in(stream_key, 6), dim), (blocks,), jnp.float32, low / len(cuts), largest / len(cuts))
        factor_of = factor_of * jnp.repeat(jnp.exp(heights), shape[dim] // blocks).reshape((-1,) + (1,) * (len(shape) - 1 - dim))
    return factor_of


def routed_block(own_key, own, number, rows, count, top, most, lean):
    sequence = jax.random.permutation(own_key, count)
    packed, common = portions_of(count, rows * top, most, lean, True), portions_of(count, rows * top, most, lean, False)
    places = jnp.arange(count)

    def named(sizes, rotation):
        used = int((sizes > 0).sum())
        fixed = max(1, used // 4)
        moved = fixed + (places - fixed + rotation * (used - fixed)) % max(1, count - fixed)
        return jnp.zeros((count,), jnp.int32).at[sequence[jnp.where(places < fixed, places, moved)]].set(jnp.asarray(sizes, jnp.int32))

    sizes = jnp.where(number % 4 == 0, named(packed, number // 4), named(common, number - number // 4 - 1))
    mixed = jax.random.permutation(jax.random.fold_in(own, 3), count)
    source_of, sink = mixed[0:count // 2 * 2:2], mixed[1:count // 2 * 2:2]
    margin = jnp.minimum(sizes[source_of] - 1, most - sizes[sink]) // 2
    margin = jnp.where((source_of == sequence[0]) | (sink == sequence[0]) | (sizes[sink] == 0), 0, jnp.maximum(margin, 0))
    moved = jax.random.randint(jax.random.fold_in(own, 4), (count // 2,), 0, 1 << 20) % (margin + 1)
    sizes = sizes.at[source_of].add(-moved).at[sink].add(moved)
    members = jnp.searchsorted(jnp.cumsum(sizes), jnp.arange(rows * top), side="right").astype(jnp.int32)
    listing = members.reshape(top, rows).T
    listing = listing[jax.random.permutation(jax.random.fold_in(own, 1), rows)]
    rotation = jax.random.randint(jax.random.fold_in(own, 2), (rows, 1), 0, top)
    return jnp.take_along_axis(listing, (jnp.arange(top)[None, :] + rotation) % top, axis=1)


def portions_of(number_of, total, bound, lean, full):
    weights = [(1 << 20) // math.isqrt(standing ** lean) + 1 for standing in range(1, number_of + 1)]
    largest = bound if full else min(bound, max(-(-total // number_of), total * weights[0] // sum(weights)))
    least = 1 if total - largest >= number_of - 1 else 0
    counts, spare = [largest] + [least] * (number_of - 1), total - largest - least * (number_of - 1)
    while spare > 0:
        movable = [i for i in range(1, number_of) if counts[i] < largest] or [i for i in range(1, number_of) if counts[i] < bound]
        pool, left = sum([weights[i] for i in movable]), spare
        for i in movable:
            extra = min(bound - counts[i], max(1, left * weights[i] // pool), spare)
            counts[i] = counts[i] + extra
            spare = spare - extra
    return np.array(counts)


def bell_draw(stream_key, dims, scale, limit, pieces=(), kind=jnp.bfloat16):
    array = jax.random.normal(stream_key, dims, jnp.float32) * scale
    if len(pieces) > 0:
        array = levels(stream_key, dims, pieces, -0.22, 0.18) * array
    return jnp.clip(array, min=-limit, max=limit).astype(kind)


def setup_inputs(seed: int = 0) -> dict:
    splits = jax.random.split(jax.random.key(seed), 14)
    hidden_in = bell_draw(splits[0], (TOKENS, D), 1.0, 6.0, ((0, 8),))
    cache_lengths = draw_cache_lengths(jax.random.fold_in(splits[13], 71), 0)
    key_cache = draw_key_cache(jax.random.fold_in(splits[13], 71), 0)
    value_cache = bell_draw(splits[3], (REQUESTS, CACHE, HD), 1.0, 6.0, ((0, 8), (2, 4)))
    attn_norm = jnp.clip(1.0 + 0.1 * jax.random.normal(splits[4], (D,), jnp.float32), 0.5, 1.5)
    w_qkv = bell_draw(splits[5], (3, D, HD), D ** -0.5, 0.125, ((2, 4),))
    w_out = bell_draw(splits[6], (HD, D), HD ** -0.5, 0.125, ((0, 4),))
    ffn_norm = jnp.clip(1.0 + 0.1 * jax.random.normal(splits[7], (D,), jnp.float32), 0.5, 1.5)
    router = bell_draw(splits[8], (D, EXPERTS), D ** -0.5, 0.125)
    routes_keys = jax.random.split(jax.random.fold_in(splits[9], 1), TOKENS // TOK)
    routes_turns = jax.random.permutation(jax.random.fold_in(splits[9], 3), TOKENS // TOK)
    routes = jax.vmap(lambda own, number: routed_block(jax.random.fold_in(splits[9], 2), own, number, TOK, EXPERTS, TOP, CAP, 1))(routes_keys, routes_turns).reshape((TOKENS, TOP))
    expert_gate = bell_draw(splits[10], (EXPERTS * SUB, D, FF // SUB), D ** -0.5, 0.125, ((0, 8), (2, 4)))
    expert_up = bell_draw(splits[11], (EXPERTS * SUB, D, FF // SUB), D ** -0.5, 0.125, ((0, 8), (2, 4)))
    expert_down = bell_draw(splits[12], (EXPERTS * SUB, FF // SUB, D), FF ** -0.5, 0.078125, ((0, 8), (1, 4)))
    return {"hidden_in": hidden_in, "cache_lengths": cache_lengths, "key_cache": key_cache, "value_cache": value_cache, "attn_norm": attn_norm, "w_qkv": w_qkv, "w_out": w_out, "ffn_norm": ffn_norm, "router": router, "routes": routes, "expert_gate": expert_gate, "expert_up": expert_up, "expert_down": expert_down}


EPSILON = 1e-05

def normalize(inputs, scale_gain):
    mean_square = lax.optimization_barrier(jnp.mean(inputs * inputs, axis=-1, keepdims=True))
    return inputs * lax.rsqrt(mean_square + EPSILON) * scale_gain

def rounded(inputs):
    return lax.optimization_barrier(inputs.astype(jnp.bfloat16))

def rotate(inputs, positions):
    half_dim = inputs.shape[-1] // 2
    frequency = jnp.exp(jnp.arange(half_dim, dtype=jnp.float32) * (-2.0 * math.log(10000.0) / inputs.shape[-1]))
    angles = positions.astype(jnp.float32)[:, None] * frequency[None, :]
    cosine = jnp.cos(angles)[:, None, :]
    sine_part = jnp.sin(angles)[:, None, :]
    lower_half = inputs[..., :half_dim]
    upper_half = inputs[..., half_dim:]
    return jnp.concatenate([lower_half * cosine - upper_half * sine_part, lower_half * sine_part + upper_half * cosine], axis=-1)

def attention(queries, all_keys, all_values, length):
    query_count = queries.shape[0]
    cache_len = all_keys.shape[0] - query_count
    scores = jnp.einsum('qhd,khd->hqk', queries.astype(jnp.float32), all_keys.astype(jnp.float32)) * queries.shape[-1] ** (-0.5)
    slot_ids = jnp.arange(cache_len + query_count, dtype=jnp.int32)
    query_ids = jnp.arange(query_count, dtype=jnp.int32)
    is_live = jnp.where(slot_ids[None, :] < cache_len, slot_ids[None, :] < length, slot_ids[None, :] - cache_len <= query_ids[:, None])
    scores = jnp.where(is_live[None], scores, -jnp.inf)
    row_max = lax.optimization_barrier(jnp.max(scores, axis=-1, keepdims=True))
    weights = jnp.exp(scores - row_max)
    totals = lax.optimization_barrier(jnp.sum(weights, axis=-1))
    mixture = jnp.einsum('hqk,khd->qhd', rounded(weights).astype(jnp.float32), all_values.astype(jnp.float32))
    return (mixture / jnp.transpose(totals)[:, :, None]).astype(jnp.bfloat16)

def reference(hidden_in, cache_lengths, key_cache, value_cache, attn_norm, w_qkv, w_out, ffn_norm, router, routes, expert_gate, expert_up, expert_down):
    residual = hidden_in.astype(jnp.float32)
    normed = rounded(normalize(residual, attn_norm))
    projection = w_qkv.astype(jnp.float32)
    local_heads = HD // HEAD

    def one_request(items):
        token_rows, length, cached_keys, cached_values = items
        projected = jnp.einsum('td,cdh->cth', token_rows.astype(jnp.float32), projection)
        positions = length + jnp.arange(TOK, dtype=jnp.int32)
        queries = rounded(rotate(projected[0].reshape(TOK, local_heads, HEAD), positions))
        fresh_keys = rounded(rotate(projected[1].reshape(TOK, local_heads, HEAD), positions))
        fresh_values = rounded(projected[2].reshape(TOK, local_heads, HEAD))
        all_keys = jnp.concatenate([cached_keys.reshape(CACHE, local_heads, HEAD), fresh_keys], axis=0)
        all_values = jnp.concatenate([cached_values.reshape(CACHE, local_heads, HEAD), fresh_values], axis=0)
        return attention(queries, all_keys, all_values, length).reshape(TOK, HD)
    attended = lax.map(one_request, (normed.reshape(REQUESTS, TOK, D), cache_lengths, key_cache, value_cache))
    attended = attended.reshape(TOKENS, HD)
    residual = residual + jnp.dot(attended, w_out, preferred_element_type=jnp.float32)
    moe_input = normalize(residual, ffn_norm).astype(jnp.bfloat16)
    logits = jnp.dot(moe_input, router, preferred_element_type=jnp.float32)
    chosen = jnp.take_along_axis(logits, routes, axis=1)
    first_gate = 1.0 / (1.0 + jnp.exp(chosen[:, 1] - chosen[:, 0]))
    second_gate = 1.0 / (1.0 + jnp.exp(chosen[:, 0] - chosen[:, 1]))
    flat_routes = routes.reshape(-1).astype(jnp.int32)
    onehot = (flat_routes[:, None] == jnp.arange(EXPERTS, dtype=jnp.int32)[None, :]).astype(jnp.int32)
    slot_rank = lax.optimization_barrier(jnp.sum((jnp.cumsum(onehot, axis=0) - onehot) * onehot, axis=1)).astype(jnp.int32)
    slot_count = N_REQ * CAP
    token_ids = (jnp.arange(TOKENS * TOP, dtype=jnp.int32) // TOP).astype(jnp.int32)
    owner = jnp.zeros((EXPERTS, slot_count), jnp.int32).at[flat_routes, slot_rank].set(token_ids)
    gate_all = expert_gate.reshape(EXPERTS, SUB, D, FF // SUB)
    up_all = expert_up.reshape(EXPERTS, SUB, D, FF // SUB)
    down_all = expert_down.reshape(EXPERTS, FF, D)
    piece_len = FF // (SUB * N_TP)

    def one_expert(items):
        owners, gate_part, up_part, down_part = items
        token_rows = moe_input[owners]
        gate_full = jnp.transpose(gate_part, (1, 0, 2)).reshape(D, FF)
        up_full = jnp.transpose(up_part, (1, 0, 2)).reshape(D, FF)
        gate_proj = jnp.dot(token_rows, gate_full, preferred_element_type=jnp.float32)
        up_proj = jnp.dot(token_rows, up_full, preferred_element_type=jnp.float32)
        activation = (jax.nn.silu(gate_proj) * up_proj).astype(jnp.bfloat16)
        totals = jnp.zeros((slot_count, D), jnp.float32)
        for slice_index in range(SUB * N_TP):
            lower = slice_index * piece_len
            partial_value = jnp.dot(activation[:, lower:lower + piece_len], down_part[lower:lower + piece_len], preferred_element_type=jnp.float32)
            totals = totals + rounded(partial_value).astype(jnp.float32)
        return totals
    results = lax.map(one_expert, (owner, gate_all, up_all, down_all))
    picked = results[flat_routes, slot_rank].reshape(TOKENS, TOP, D)
    mixed_out = first_gate[:, None] * picked[:, 0] + second_gate[:, None] * picked[:, 1]
    return (residual + mixed_out).astype(jnp.bfloat16)
```

```python
import functools
import math

import jax
import jax.numpy as jnp
from jax import lax
from jax.experimental import pallas as pl
from jax.experimental.pallas import tpu as pltpu
from jax.sharding import PartitionSpec as P

HEAD = 64
TOP = 2
CAP = 96
PACK = 16
SLICE = 256
MASKED = -1e30
EPSILON = 1e-05
NT = (((1,), (1,)), ((), ()))


def normalize(inputs, scale_gain):
    mean_square = jnp.mean(inputs * inputs, axis=-1, keepdims=True)
    return inputs * lax.rsqrt(mean_square + EPSILON) * scale_gain


def rotate_rows(inputs, cosine, sine_part):
    half_dim = inputs.shape[0] // 2
    lower_half = inputs[:half_dim]
    upper_half = inputs[half_dim:]
    return jnp.concatenate(
        [
            lower_half * cosine - upper_half * sine_part,
            lower_half * sine_part + upper_half * cosine,
        ],
        axis=0,
    )


def scores_of(first, count, length, shift, tokens, q, kc, kf):
    cache_len = kc.shape[1]
    slots = lax.broadcasted_iota(jnp.int32, (PACK, cache_len), 1)
    top_row = lax.broadcasted_iota(jnp.int32, (PACK, cache_len), 0) == 0
    bias = jnp.where(top_row & (slots >= length), MASKED, 0.0).astype(jnp.bfloat16)
    s_c = jnp.dot(q, jnp.concatenate([kc, bias], axis=0), preferred_element_type=jnp.float32)
    pad = jnp.zeros((PACK, kf.shape[1]), kf.dtype)
    s_f = jnp.dot(q, jnp.concatenate([kf, pad], axis=0), preferred_element_type=jnp.float32)
    row = lax.rem(lax.broadcasted_iota(jnp.int32, (count, 1), 0) + (first + shift), tokens)
    col = lax.rem(lax.broadcasted_iota(jnp.int32, (1, tokens), 1) + shift, tokens)
    return s_c, jnp.where(col <= row, s_f, MASKED)


def mixture(scores, vc, vf):
    s_c, s_f = scores
    top = jnp.maximum(jnp.max(s_c, axis=1, keepdims=True), jnp.max(s_f, axis=1, keepdims=True))
    p_c = jnp.exp(s_c - top)
    p_f = jnp.exp(s_f - top)
    totals = jnp.sum(p_c, axis=1, keepdims=True) + jnp.sum(p_f, axis=1, keepdims=True)
    mixed = lax.dot_general(p_c.astype(jnp.bfloat16), vc, NT, preferred_element_type=jnp.float32)
    mixed = mixed + lax.dot_general(
        p_f.astype(jnp.bfloat16), vf, NT, preferred_element_type=jnp.float32
    )
    return mixed / totals


def attend_heads(heads, make_scores, make_mixture, attended):
    mixed = []
    ahead = make_scores(0)
    for g in range(heads):
        now = ahead
        if g + 1 < heads:
            ahead = make_scores(g + 1)
        mixed.append(make_mixture(g, now))
    attended[pl.program_id(0)] = jnp.concatenate(mixed, axis=1).astype(jnp.bfloat16)


def widened(q):
    count = q.shape[1]
    ones = jnp.where(lax.broadcasted_iota(jnp.int32, (PACK, count), 0) == 0, 1.0, 0.0)
    return jnp.concatenate([q, ones], axis=0).T.astype(jnp.bfloat16)


def head_slice(g):
    return slice(g * HEAD, (g + 1) * HEAD)


def attention_kernel(
    share,
    scalars,
    hidden_ref,
    gain_ref,
    w_ref,
    cos_ref,
    sin_ref,
    kc_ref,
    vc_ref,
    wo_ref,
    *rest,
):
    *out_refs, normed, attended, total = rest
    tokens, width = hidden_ref.shape
    blocks = tokens // share
    rows_here = kc_ref.shape[0]
    heads = rows_here // HEAD
    length, shift = scalars[0], scalars[1] * share

    @pl.when(pl.program_id(0) == 0)
    def _():
        for k in range(0, blocks, 2):
            pair = []
            for i in range(2):
                start = pl.multiple_of(lax.rem(scalars[1] + k + i, blocks) * share, share)
                rows = hidden_ref[pl.ds(start, share), :].astype(jnp.float32)
                pair.append(normalize(rows, gain_ref[...]))
            normed[:, k * share : (k + 2) * share] = jnp.concatenate(pair, axis=0).T.astype(
                jnp.bfloat16
            )

    weights = w_ref[...].reshape(3 * rows_here, width)
    projected = jnp.dot(weights, normed[...], preferred_element_type=jnp.float32)
    cosine, sine_part = cos_ref[...], sin_ref[...]

    def make_scores(g):
        q = rotate_rows(projected[head_slice(g)], cosine, sine_part).astype(jnp.bfloat16)
        q = widened(q.astype(jnp.float32) * HEAD**-0.5)
        kf = rotate_rows(projected[head_slice(heads + g)], cosine, sine_part).astype(jnp.bfloat16)
        return scores_of(0, tokens, length, shift, tokens, q, kc_ref[head_slice(g), :], kf)

    def make_mixture(g, scores):
        vf = projected[head_slice(2 * heads + g)].astype(jnp.bfloat16)
        return mixture(scores, vc_ref[head_slice(g), :], vf)

    attend_heads(heads, make_scores, make_mixture, attended)

    @pl.when(pl.program_id(0) == pl.num_programs(0) - 1)
    def _():
        steps = attended.shape[0]
        total[...] = sum(
            jnp.dot(
                attended[i],
                wo_ref[i * rows_here : (i + 1) * rows_here, :],
                preferred_element_type=jnp.float32,
            )
            for i in range(steps)
        )
        for i, out_ref in enumerate(out_refs):
            ahead = (i + 1) % blocks
            first = width - blocks * SLICE
            place = lax.rem(scalars[1] + i, blocks) * SLICE + first
            lanes = pl.ds(pl.multiple_of(place, SLICE), SLICE)
            out_ref[:, :first] = total[i * share : (i + 1) * share, :first].astype(out_ref.dtype)
            for j in range(blocks):
                start = (ahead + j - 1) % blocks * share
                out_ref[:, first + j * SLICE : first + (j + 1) * SLICE] = total[
                    start : start + share, lanes
                ].astype(out_ref.dtype)


def merge_kernel(share, pieces, scalars, *refs):
    piece_refs = refs[:pieces]
    hidden_ref, gain_ref, router_ref = refs[pieces : pieces + 3]
    first_ref, slice_ref, first_raw_ref, slice_raw_ref, *term_refs = refs[pieces + 3 :]
    tp = len(term_refs)
    me = scalars[0]
    first = first_ref.shape[1]
    exact = functools.partial(
        lax.dot_general,
        dimension_numbers=NT,
        precision=lax.Precision.HIGHEST,
        preferred_element_type=jnp.float32,
    )

    def terms_of(rows, lanes):
        weights = router_ref[:, lanes].astype(jnp.float32) * gain_ref[:, lanes]
        return jnp.concatenate(
            [exact(weights, rows), exact(jnp.ones_like(weights), rows * rows)], axis=0
        )

    def block_start(j):
        return pl.multiple_of(lax.rem(me + j, tp) * share, share)

    total = piece_refs[0][...].astype(jnp.float32)
    for ref in piece_refs[1:]:
        total = total + ref[...].astype(jnp.float32)
    own = hidden_ref[pl.ds(block_start(0), share), :first].astype(jnp.float32) + total[:, :first]
    first_ref[...] = own
    first_raw_ref[...] = own.astype(jnp.bfloat16)
    lanes = pl.ds(pl.multiple_of(first + me * SLICE, SLICE), SLICE)
    terms = []
    for j in range(tp):
        rows = hidden_ref[pl.ds(block_start(j), share), lanes].astype(jnp.float32)
        rows = rows + total[:, first + j * SLICE : first + (j + 1) * SLICE]
        slice_ref[j * share : (j + 1) * share, :] = rows
        slice_raw_ref[j * share : (j + 1) * share, :] = rows.astype(jnp.bfloat16)
        terms.append(terms_of(rows, lanes))
    terms[0] = terms[0] + terms_of(own, slice(0, first))
    for k in range(tp):
        for j in range(tp):
            term_refs[k][j] = terms[(j + k) % tp]


def merge(me_tp, pieces, hidden_in, gain, router_t):
    share, width = pieces[0].shape
    tp = len(pieces)
    tokens = hidden_in.shape[0]
    first = width - tp * SLICE
    experts = router_t.shape[0]
    terms = jax.ShapeDtypeStruct((tp, 2 * experts, share), jnp.float32)
    return pl.pallas_call(
        functools.partial(merge_kernel, share, tp),
        grid_spec=pltpu.PrefetchScalarGridSpec(
            num_scalar_prefetch=1,
            grid=(1,),
            in_specs=[pl.BlockSpec(p.shape, lambda i, s: (0, 0)) for p in pieces]
            + [pl.BlockSpec(a.shape, lambda i, s: (0, 0)) for a in (hidden_in, gain, router_t)],
            out_specs=[
                pl.BlockSpec((share, first), lambda i, s: (0, 0)),
                pl.BlockSpec((tokens, SLICE), lambda i, s: (0, 0)),
            ]
            * 2
            + [pl.BlockSpec(terms.shape, lambda i, s: (0, 0, 0))] * tp,
        ),
        out_shape=[
            jax.ShapeDtypeStruct((share, first), jnp.float32),
            jax.ShapeDtypeStruct((tokens, SLICE), jnp.float32),
            jax.ShapeDtypeStruct((share, first), jnp.bfloat16),
            jax.ShapeDtypeStruct((tokens, SLICE), jnp.bfloat16),
        ]
        + [terms] * tp,
        compiler_params=pltpu.CompilerParams(vmem_limit_bytes=32 * 1024 * 1024),
        cost_estimate=pl.CostEstimate(
            flops=8 * tp * share * width,
            bytes_accessed=2 * tokens * width + 4 * share * width * tp,
            transcendentals=0,
        ),
    )(me_tp.reshape(1), *pieces, hidden_in, gain, router_t)


def assemble_kernel(slices, scalars, first_ref, *refs):
    slice_refs = refs[:slices]
    gain_ref, out_ref = refs[slices:]
    first = first_ref.shape[1]
    width = out_ref.shape[1]
    rows = first_ref[...].astype(jnp.float32)
    parts = [ref[...].astype(jnp.float32) for ref in slice_refs]
    squares = jnp.sum(rows * rows, axis=1, keepdims=True)
    for part in parts:
        squares = squares + jnp.sum(part * part, axis=1, keepdims=True)
    scale = lax.rsqrt(squares / width + EPSILON)
    out_ref[:, :first] = (rows * scale * gain_ref[:, :first]).astype(jnp.bfloat16)
    for k, part in enumerate(parts):
        place = lax.rem(scalars[0] + k, slices) * SLICE + first
        lanes = pl.ds(pl.multiple_of(place, SLICE), SLICE)
        out_ref[:, lanes] = (part * scale * gain_ref[:, lanes]).astype(jnp.bfloat16)


def assemble(me_tp, first_rows, slices, gain):
    rows, first = first_rows.shape
    width = first + SLICE * len(slices)
    tile = 2 * CAP

    def tiles(n):
        return pl.BlockSpec((tile, n), lambda i, s: (i, 0))

    return pl.pallas_call(
        functools.partial(assemble_kernel, len(slices)),
        grid_spec=pltpu.PrefetchScalarGridSpec(
            num_scalar_prefetch=1,
            grid=(rows // tile,),
            in_specs=[tiles(first)]
            + [tiles(SLICE)] * len(slices)
            + [pl.BlockSpec((1, width), lambda i, s: (0, 0))],
            out_specs=tiles(width),
        ),
        out_shape=jax.ShapeDtypeStruct((rows, width), jnp.bfloat16),
        compiler_params=pltpu.CompilerParams(vmem_limit_bytes=16 * 1024 * 1024),
        cost_estimate=pl.CostEstimate(
            flops=8 * rows * width, bytes_accessed=4 * rows * width, transcendentals=rows
        ),
    )(me_tp.reshape(1), first_rows, *slices, gain)


def combine_kernel(width, copies, terms, rows_ref, routes_ref, places_ref, base_ref, *refs):
    term_refs, out_refs = refs[:terms], refs[terms:]
    tp = len(out_refs)
    total = term_refs[0][...]
    for ref in term_refs[1:]:
        total = total + ref[...]
    experts = total.shape[1] // 2
    total = jnp.concatenate([total[j] for j in range(tp)], axis=1).T
    tokens = total.shape[0]
    share = tokens // tp
    scale = lax.rsqrt(total[:, experts : experts + 1] / width + EPSILON)
    logits = total[:, :experts] * scale
    ids = lax.broadcasted_iota(jnp.int32, (tokens, experts), 1)
    slots = lax.broadcasted_iota(jnp.int32, (tokens, rows_ref.shape[0]), 1)
    rows = rows_ref[...]
    chosen, picked = [], []
    for k in range(TOP):
        match = routes_ref[:, k : k + 1] == ids
        chosen.append(jnp.sum(jnp.where(match, logits, 0.0), axis=1, keepdims=True))
        place = places_ref[:, k : k + 1]
        hit = slots == place
        for c in range(1, copies):
            hit = hit | (slots == place + c * CAP)
        picked.append(
            jnp.dot(
                jnp.where(hit, 1.0, 0.0).astype(jnp.bfloat16),
                rows,
                preferred_element_type=jnp.float32,
            )
        )
    first_gate = 1.0 / (1.0 + jnp.exp(chosen[1] - chosen[0]))
    second_gate = 1.0 / (1.0 + jnp.exp(chosen[0] - chosen[1]))
    mixed = first_gate * picked[0] + second_gate * picked[1]
    for k, out_ref in enumerate(out_refs):
        block = mixed[k * share : (k + 1) * share]
        if k * share < base_ref.shape[0]:
            block = block + base_ref[k * share : (k + 1) * share, :]
        out_ref[...] = block.astype(out_ref.dtype)


def combine(width, copies, rows, routes, places, base, terms, kinds):
    tokens = routes.shape[0]
    share = tokens // len(kinds)
    columns = rows.shape[1]

    def full(array):
        return pl.BlockSpec(array.shape, lambda i: (0,) * array.ndim)

    operands = [rows, routes, places, base, *terms]
    return pl.pallas_call(
        functools.partial(combine_kernel, width, copies, len(terms)),
        grid=(1,),
        in_specs=[full(a) for a in operands],
        out_specs=[pl.BlockSpec((share, columns), lambda i: (0, 0))] * len(kinds),
        out_shape=[jax.ShapeDtypeStruct((share, columns), kind) for kind in kinds],
        compiler_params=pltpu.CompilerParams(vmem_limit_bytes=40 * 1024 * 1024),
        cost_estimate=pl.CostEstimate(
            flops=4 * tokens * rows.shape[0] * columns,
            bytes_accessed=2 * rows.shape[0] * columns + 8 * tokens * columns,
            transcendentals=4 * tokens,
        ),
    )(*operands)


def per_device(
    hidden_in,
    cache_lengths,
    key_cache,
    value_cache,
    attn_norm,
    w_qkv,
    w_out,
    ffn_norm,
    router,
    routes,
    expert_gate,
    expert_up,
    expert_down,
):
    token_count, model_width = hidden_in.shape
    local_lanes = w_qkv.shape[2]
    local_heads = local_lanes // HEAD
    cache_len = key_cache.shape[1]
    tp = lax.axis_size("tp")
    me_tp = lax.axis_index("tp")
    req = lax.axis_size("req")
    expert_count = router.shape[1]
    copies = req // expert_count
    share = token_count // tp
    first_width = model_width - tp * SLICE

    def to_block(array, k):
        return lax.ppermute(array, "tp", [(i, (i + k) % tp) for i in range(tp)])

    def from_block(array, k):
        return lax.ppermute(array, "tp", [(i, (i - k) % tp) for i in range(tp)])

    def exchanged(rows):
        blocks = rows.reshape(req, CAP, -1)
        blocks = lax.all_to_all(blocks, "req", split_axis=0, concat_axis=0, tiled=True)
        return blocks.reshape(req * CAP, -1)

    def to_experts(tokens):
        packed = jnp.dot(placing, tokens, preferred_element_type=jnp.float32).astype(jnp.bfloat16)
        packed = packed.reshape(expert_count, 1, CAP, -1)
        return exchanged(
            jnp.broadcast_to(packed, (expert_count, copies, CAP, packed.shape[-1]))
        )

    def from_own(array):
        twice = jnp.concatenate([array, array], axis=0)
        return lax.dynamic_slice_in_dim(twice, me_tp * share, token_count, 0)

    expert_ids = jnp.arange(expert_count, dtype=jnp.int32)
    has = jnp.any(routes[:, :, None] == expert_ids[None, None, :], axis=1)
    token_ids = jnp.arange(token_count, dtype=jnp.int32)
    earlier = (token_ids[None, :] < token_ids[:, None]).astype(jnp.bfloat16)
    rank = jnp.dot(earlier, has.astype(jnp.bfloat16), preferred_element_type=jnp.float32).astype(
        jnp.int32
    )
    slot = from_own(jnp.where(has, rank, -1))
    rolled = from_own(routes)
    named = rolled[:, :, None] == expert_ids[None, None, :]
    slots = jnp.arange(CAP, dtype=jnp.int32)
    placing = (
        (slot.T[:, None, :] == slots[None, :, None])
        .astype(jnp.bfloat16)
        .reshape(expert_count * CAP, token_count)
    )
    places = jnp.sum(jnp.where(named, slot[:, None, :], 0), axis=2) + rolled * (copies * CAP)

    length = cache_lengths[0]
    scalars = jnp.stack([length, (me_tp + 1) % tp]).astype(jnp.int32)
    positions = length + (token_ids + scalars[1] * share) % token_count
    positions = positions.astype(jnp.float32)
    half = HEAD // 2
    frequency = jnp.exp(jnp.arange(half, dtype=jnp.float32) * (-2.0 * math.log(10000.0) / HEAD))
    angles = frequency[:, None] * positions[None, :]
    cosine = jnp.cos(angles)
    sine_part = jnp.sin(angles)
    keys_t = jnp.swapaxes(key_cache[0], 0, 1)
    values_t = jnp.swapaxes(value_cache[0], 0, 1)
    w_t = jnp.swapaxes(w_qkv, 1, 2)
    group = 3 if local_heads % 3 == 0 else 1

    def whole(*shape):
        return pl.BlockSpec(shape, lambda h, s: (0,) * len(shape))

    def head_rows(n):
        return pl.BlockSpec((group * HEAD, n), lambda h, s: (h, 0))

    *sent, own_partial = pl.pallas_call(
        functools.partial(attention_kernel, share),
        grid_spec=pltpu.PrefetchScalarGridSpec(
            num_scalar_prefetch=1,
            grid=(local_heads // group,),
            in_specs=[
                whole(token_count, model_width),
                whole(model_width),
                pl.BlockSpec((3, group * HEAD, model_width), lambda h, s: (0, h, 0)),
                whole(half, token_count),
                whole(half, token_count),
                head_rows(cache_len),
                head_rows(cache_len),
                whole(local_lanes, model_width),
            ],
            out_specs=[whole(share, model_width)] * tp,
            scratch_shapes=[
                pltpu.VMEM((model_width, token_count), jnp.bfloat16),
                pltpu.VMEM((local_heads // group, token_count, group * HEAD), jnp.bfloat16),
                pltpu.VMEM((token_count, model_width), jnp.float32),
            ],
        ),
        out_shape=[jax.ShapeDtypeStruct((share, model_width), jnp.bfloat16)] * tp,
        compiler_params=pltpu.CompilerParams(vmem_limit_bytes=62 * 1024 * 1024),
        cost_estimate=pl.CostEstimate(
            flops=token_count * local_lanes * (8 * model_width + 4 * (cache_len + token_count)),
            bytes_accessed=2 * local_lanes * (4 * model_width + 2 * cache_len),
            transcendentals=token_count * (cache_len + token_count) * local_heads,
        ),
    )(
        scalars,
        hidden_in,
        attn_norm,
        w_t,
        cosine,
        sine_part,
        keys_t,
        values_t,
        w_out,
    )
    arrived = [to_block(piece, k + 1) for k, piece in enumerate(sent)]

    gain = ffn_norm.reshape(1, model_width)
    first_residual, slice_residual, first_raw, slice_raw, *terms = merge(
        me_tp, [own_partial, *arrived], hidden_in, gain, jnp.swapaxes(router, 0, 1)
    )

    slice_downs = lax.optimization_barrier(
        [
            lax.dynamic_slice_in_dim(
                expert_down[0], first_width + (me_tp + k) % tp * SLICE, SLICE, 1
            )
            for k in range(tp)
        ]
    )

    gathered = jnp.concatenate(
        [first_raw] + [from_block(first_raw, k) for k in range(1, tp)], axis=0
    )
    slice_rows = to_experts(slice_raw)

    first_rows = to_experts(gathered)
    slices = [slice_rows] + [from_block(slice_rows, k) for k in range(1, tp)]
    token_rows = assemble(me_tp, first_rows, slices, gain)

    token_rows, *terms = lax.optimization_barrier((token_rows, *terms))
    terms = [terms[0]] + [to_block(terms[k], k) for k in range(1, tp)]

    gate_proj = jnp.dot(token_rows, expert_gate[0], preferred_element_type=jnp.float32)
    up_proj = jnp.dot(token_rows, expert_up[0], preferred_element_type=jnp.float32)
    activation = (jax.nn.silu(gate_proj) * up_proj).astype(jnp.bfloat16)
    activation = lax.optimization_barrier(activation)

    def down(rows, weights):
        return jnp.dot(rows, weights, preferred_element_type=jnp.float32).astype(jnp.bfloat16)

    slice_terms = lax.optimization_barrier([down(activation, w) for w in slice_downs])
    coming = [to_block(slice_terms[k], k) for k in range(1, tp)]
    activation, _ = lax.optimization_barrier((activation, slice_terms[tp - 1]))
    first_back = exchanged(down(activation, expert_down[0, :, :first_width]))
    slice_sum = slice_terms[0].astype(jnp.float32)
    for term in coming:
        slice_sum = slice_sum + term.astype(jnp.float32)
    slice_sum, first_back = lax.optimization_barrier((slice_sum.astype(jnp.bfloat16), first_back))

    kinds = [jnp.bfloat16] * tp
    first_out, *first_shares = combine(
        model_width,
        copies,
        first_back,
        rolled,
        places,
        first_residual,
        terms,
        [jnp.float32, *kinds[1:]],
    )
    for k, piece in enumerate(first_shares):
        first_out = first_out + to_block(piece, k + 1).astype(jnp.float32)
    slice_outs = combine(
        model_width,
        copies,
        exchanged(slice_sum),
        rolled,
        places,
        slice_residual,
        terms,
        kinds,
    )
    slice_outs = [slice_outs[0]] + [to_block(slice_outs[k], k) for k in range(1, tp)]
    slice_outs = jnp.stack(slice_outs[::-1] * 2)
    slice_outs = lax.dynamic_slice_in_dim(slice_outs, (2 * tp - 1 - me_tp) % tp, tp, 0)
    return jnp.concatenate(
        [first_out.astype(jnp.bfloat16)] + [slice_outs[j] for j in range(tp)], axis=1
    )


def solution(mesh):
    return jax.shard_map(
        per_device,
        mesh=mesh,
        in_specs=(
            P("req", None),
            P("req"),
            P("req", None, "tp"),
            P("req", None, "tp"),
            P(),
            P(None, None, "tp"),
            P("tp", None),
            P(),
            P(),
            P("req", None),
            P("req", None, "tp"),
            P("req", None, "tp"),
            P("req", "tp", None),
        ),
        out_specs=P(("req", "tp"), None),
        check_vma=False,
    )
```

```python
import functools
import math

import jax
import jax.numpy as jnp
from jax import lax
from jax.experimental import pallas as pl
from jax.experimental.pallas import tpu as pltpu
from jax.sharding import PartitionSpec as P

HEAD = 64
TOP = 2
CAP = 96
PACK = 16
KEYS = 256
SLICE = 256
MASKED = -1e30
EPSILON = 1e-05
NT = (((1,), (1,)), ((), ()))
AHEAD = pl.CostEstimate(flops=1 << 37, bytes_accessed=1 << 20, transcendentals=0)


def normalize(inputs, scale_gain):
    mean_square = jnp.mean(inputs * inputs, axis=-1, keepdims=True)
    return inputs * lax.rsqrt(mean_square + EPSILON) * scale_gain


def rotate_rows(inputs, cosine, sine_part):
    half_dim = inputs.shape[0] // 2
    lower_half = inputs[:half_dim]
    upper_half = inputs[half_dim:]
    return jnp.concatenate(
        [
            lower_half * cosine - upper_half * sine_part,
            lower_half * sine_part + upper_half * cosine,
        ],
        axis=0,
    )


def lane_halves(chunk, join):
    half = chunk.shape[1] // 2
    return join(chunk[:, :half], chunk[:, half:])


def attend_heads(heads, chunks, score, value):
    def row_top(scores):
        top = lane_halves(scores[0], jnp.maximum)
        for chunk in scores[1:]:
            top = jnp.maximum(top, lane_halves(chunk, jnp.maximum))
        return jnp.max(top, axis=1, keepdims=True)

    outputs = []
    ahead = [score(0, c) for c in range(chunks)]
    for g in range(heads):
        now, ahead = ahead, []
        top = row_top(now)
        totals = mixed = None
        for c in range(chunks):
            if g + 1 < heads:
                ahead.append(score(g + 1, c))
            probs = jnp.exp(now[c] - top)
            part = lane_halves(probs, jnp.add)
            totals = part if totals is None else totals + part
            part = lax.dot_general(
                probs.astype(jnp.bfloat16), value(g, c), NT, preferred_element_type=jnp.float32
            )
            mixed = part if mixed is None else mixed + part
        outputs.append(mixed / jnp.sum(totals, axis=1, keepdims=True))
    return outputs


def widened(q):
    count = q.shape[1]
    ones = jnp.where(lax.broadcasted_iota(jnp.int32, (PACK, count), 0) == 0, 1.0, 0.0)
    return jnp.concatenate([q, ones], axis=0).T.astype(jnp.bfloat16)


def head_slice(g):
    return slice(g * HEAD, (g + 1) * HEAD)


def attention_kernel(
    share,
    scalars,
    hidden_ref,
    gain_ref,
    w_ref,
    cos_ref,
    sin_ref,
    kc_ref,
    vc_ref,
    wo_ref,
    *rest,
):
    *out_refs, normed, attended, total = rest
    tokens, width = hidden_ref.shape
    blocks = tokens // share
    rows_here = kc_ref.shape[0]
    heads = rows_here // HEAD
    length, shift = scalars[0], scalars[1] * share

    @pl.when(pl.program_id(0) == 0)
    def _():
        for k in range(0, blocks, 2):
            pair = []
            for i in range(2):
                start = pl.multiple_of(lax.rem(scalars[1] + k + i, blocks) * share, share)
                rows = hidden_ref[pl.ds(start, share), :].astype(jnp.float32)
                pair.append(normalize(rows, gain_ref[...]))
            normed[:, k * share : (k + 2) * share] = jnp.concatenate(pair, axis=0).T.astype(
                jnp.bfloat16
            )

    weights = w_ref[...].reshape(3 * rows_here, width)
    projected = jnp.dot(weights, normed[...], preferred_element_type=jnp.float32)
    cosine, sine_part = cos_ref[...], sin_ref[...]

    cache_len = kc_ref.shape[1]
    cached = cache_len // KEYS
    pad = jnp.zeros((PACK, tokens), jnp.bfloat16)
    queries, keys, values = [], [], []
    for g in range(heads):
        q = rotate_rows(projected[head_slice(g)], cosine, sine_part).astype(jnp.bfloat16)
        queries.append(widened(q.astype(jnp.float32) * HEAD**-0.5))
        kf = rotate_rows(projected[head_slice(heads + g)], cosine, sine_part).astype(jnp.bfloat16)
        keys.append(jnp.concatenate([kf, pad], axis=0))
        values.append(projected[head_slice(2 * heads + g)].astype(jnp.bfloat16))
    slots = lax.broadcasted_iota(jnp.int32, (PACK, KEYS), 1)
    top_row = lax.broadcasted_iota(jnp.int32, (PACK, KEYS), 0) == 0
    row = lax.rem(lax.broadcasted_iota(jnp.int32, (tokens, 1), 0) + shift, tokens)
    col = lax.rem(lax.broadcasted_iota(jnp.int32, (1, tokens), 1) + shift, tokens)

    def chunk_of(c):
        return slice(c * KEYS, (c + 1) * KEYS)

    def score(g, c):
        if c == cached:
            scores = jnp.dot(queries[g], keys[g], preferred_element_type=jnp.float32)
            return jnp.where(col <= row, scores, MASKED)
        dead = top_row & (slots + c * KEYS >= length)
        bias = jnp.where(dead, MASKED, 0.0).astype(jnp.bfloat16)
        kc = jnp.concatenate([kc_ref[head_slice(g), chunk_of(c)], bias], axis=0)
        return jnp.dot(queries[g], kc, preferred_element_type=jnp.float32)

    def value(g, c):
        return values[g] if c == cached else vc_ref[head_slice(g), chunk_of(c)]

    outputs = attend_heads(heads, cached + 1, score, value)
    attended[pl.program_id(0)] = jnp.concatenate(outputs, axis=1).astype(jnp.bfloat16)

    @pl.when(pl.program_id(0) == pl.num_programs(0) - 1)
    def _():
        steps = attended.shape[0]
        total[...] = sum(
            jnp.dot(
                attended[i],
                wo_ref[i * rows_here : (i + 1) * rows_here, :],
                preferred_element_type=jnp.float32,
            )
            for i in range(steps)
        )
        for i, out_ref in enumerate(out_refs):
            ahead = (i + 1) % blocks
            first = width - blocks * SLICE
            place = lax.rem(scalars[1] + i, blocks) * SLICE + first
            lanes = pl.ds(pl.multiple_of(place, SLICE), SLICE)
            out_ref[:, :first] = total[i * share : (i + 1) * share, :first].astype(out_ref.dtype)
            for j in range(blocks):
                start = (ahead + j - 1) % blocks * share
                out_ref[:, first + j * SLICE : first + (j + 1) * SLICE] = total[
                    start : start + share, lanes
                ].astype(out_ref.dtype)


def merge_kernel(share, pieces, scalars, *refs):
    piece_refs = refs[:pieces]
    hidden_ref, gain_ref, router_ref = refs[pieces : pieces + 3]
    first_ref, slice_ref, slice_raw_ref, *message_refs = refs[pieces + 3 :]
    tp = len(message_refs)
    me = scalars[0]
    first = first_ref.shape[1]
    exact = functools.partial(
        lax.dot_general,
        dimension_numbers=NT,
        precision=lax.Precision.HIGHEST,
        preferred_element_type=jnp.float32,
    )

    def terms_of(rows, lanes):
        weights = router_ref[:, lanes].astype(jnp.float32) * gain_ref[:, lanes]
        return exact(weights, rows), exact(jnp.ones_like(weights), rows * rows)

    def in_parts(logits, squares):
        row = lax.broadcasted_iota(jnp.int32, squares.shape, 0)
        last = jnp.zeros_like(squares)
        parts = []
        for p in range(3):
            part = logits.astype(jnp.bfloat16).astype(jnp.float32)
            logits = logits - part
            parts.append(part)
            part = squares.astype(jnp.bfloat16).astype(jnp.float32)
            squares = squares - part
            last = jnp.where(row == p, part, last)
        return jnp.concatenate([*parts, last], axis=0)

    def block_start(j):
        return pl.multiple_of(lax.rem(me + j, tp) * share, share)

    total = piece_refs[0][...].astype(jnp.float32)
    for ref in piece_refs[1:]:
        total = total + ref[...].astype(jnp.float32)
    own = hidden_ref[pl.ds(block_start(0), share), :first].astype(jnp.float32) + total[:, :first]
    first_ref[...] = own
    lanes = pl.ds(pl.multiple_of(first + me * SLICE, SLICE), SLICE)
    terms = []
    for j in range(tp):
        rows = hidden_ref[pl.ds(block_start(j), share), lanes].astype(jnp.float32)
        rows = rows + total[:, first + j * SLICE : first + (j + 1) * SLICE]
        slice_ref[j * share : (j + 1) * share, :] = rows
        slice_raw_ref[j * share : (j + 1) * share, :] = rows.astype(jnp.bfloat16)
        terms.append(terms_of(rows, lanes))
    terms[0] = [a + b for a, b in zip(terms[0], terms_of(own, slice(0, first)))]
    terms = [in_parts(*t) for t in terms]
    for k, message_ref in enumerate(message_refs):
        message_ref[:, :first] = own.astype(jnp.bfloat16)
        told = jnp.concatenate([terms[(j - k) % tp] for j in range(tp)], axis=0)
        message_ref[:, first:] = told.T.astype(jnp.bfloat16)


def merge(me_tp, pieces, hidden_in, gain, router_t):
    share, width = pieces[0].shape
    tp = len(pieces)
    tokens = hidden_in.shape[0]
    first = width - tp * SLICE
    length = first + tp * 4 * router_t.shape[0]
    return pl.pallas_call(
        functools.partial(merge_kernel, share, tp),
        grid_spec=pltpu.PrefetchScalarGridSpec(
            num_scalar_prefetch=1,
            grid=(1,),
            in_specs=[pl.BlockSpec(p.shape, lambda i, s: (0, 0)) for p in pieces]
            + [pl.BlockSpec(a.shape, lambda i, s: (0, 0)) for a in (hidden_in, gain, router_t)],
            out_specs=[
                pl.BlockSpec((share, first), lambda i, s: (0, 0)),
                pl.BlockSpec((tokens, SLICE), lambda i, s: (0, 0)),
                pl.BlockSpec((tokens, SLICE), lambda i, s: (0, 0)),
            ]
            + [pl.BlockSpec((share, length), lambda i, s: (0, 0))] * tp,
        ),
        out_shape=[
            jax.ShapeDtypeStruct((share, first), jnp.float32),
            jax.ShapeDtypeStruct((tokens, SLICE), jnp.float32),
            jax.ShapeDtypeStruct((tokens, SLICE), jnp.bfloat16),
        ]
        + [jax.ShapeDtypeStruct((share, length), jnp.bfloat16)] * tp,
        compiler_params=pltpu.CompilerParams(vmem_limit_bytes=32 * 1024 * 1024),
        cost_estimate=pl.CostEstimate(
            flops=8 * tp * share * width,
            bytes_accessed=2 * tokens * width + 4 * share * width * tp,
            transcendentals=0,
        ),
    )(me_tp.reshape(1), *pieces, hidden_in, gain, router_t)


def assemble_kernel(first_ref, rest_ref, gain_ref, out_ref):
    first = first_ref.shape[1]
    width = out_ref.shape[1]
    rows = first_ref[...].astype(jnp.float32)
    rest = rest_ref[...].astype(jnp.float32)
    squares = jnp.sum(rows * rows, axis=1, keepdims=True)
    squares = squares + jnp.sum(rest * rest, axis=1, keepdims=True)
    scale = lax.rsqrt(squares / width + EPSILON)
    out_ref[:, :first] = (rows * scale * gain_ref[:, :first]).astype(jnp.bfloat16)
    out_ref[:, first:] = (rest * scale * gain_ref[:, first:]).astype(jnp.bfloat16)


def assemble(first_rows, rest, gain):
    rows, first = first_rows.shape
    width = first + rest.shape[1]
    tile = 2 * CAP

    def tiles(n):
        return pl.BlockSpec((tile, n), lambda i: (i, 0))

    return pl.pallas_call(
        assemble_kernel,
        grid=(rows // tile,),
        in_specs=[tiles(first), tiles(width - first), pl.BlockSpec((1, width), lambda i: (0, 0))],
        out_specs=tiles(width),
        out_shape=jax.ShapeDtypeStruct((rows, width), jnp.bfloat16),
        compiler_params=pltpu.CompilerParams(vmem_limit_bytes=16 * 1024 * 1024),
        cost_estimate=pl.CostEstimate(
            flops=8 * rows * width, bytes_accessed=4 * rows * width, transcendentals=rows
        ),
    )(first_rows, rest, gain)


def combine_kernel(width, copies, terms, rows_ref, routes_ref, places_ref, base_ref, *refs):
    term_refs, out_refs = refs[:terms], refs[terms:]
    tp = len(out_refs)
    total = term_refs[0][...].astype(jnp.float32)
    for ref in term_refs[1:]:
        total = total + ref[...].astype(jnp.float32)
    share = total.shape[0]
    tokens = tp * share
    experts = total.shape[1] // (4 * tp)
    logits = []
    for j in range(tp):
        start = 4 * experts * j
        group = [total[:, start + p * experts : start + (p + 1) * experts] for p in range(4)]
        squares = group[3][:, 0:1] + group[3][:, 1:2] + group[3][:, 2:3]
        logits.append((group[0] + group[1] + group[2]) * lax.rsqrt(squares / width + EPSILON))
    logits = jnp.concatenate(logits, axis=0)
    ids = lax.broadcasted_iota(jnp.int32, (tokens, experts), 1)
    slots = lax.broadcasted_iota(jnp.int32, (tokens, rows_ref.shape[0]), 1)
    rows = rows_ref[...]
    chosen, picked = [], []
    for k in range(TOP):
        match = routes_ref[:, k : k + 1] == ids
        chosen.append(jnp.sum(jnp.where(match, logits, 0.0), axis=1, keepdims=True))
        place = places_ref[:, k : k + 1]
        hit = slots == place
        for c in range(1, copies):
            hit = hit | (slots == place + c * CAP)
        picked.append(
            jnp.dot(
                jnp.where(hit, 1.0, 0.0).astype(jnp.bfloat16),
                rows,
                preferred_element_type=jnp.float32,
            )
        )
    first_gate = 1.0 / (1.0 + jnp.exp(chosen[1] - chosen[0]))
    second_gate = 1.0 / (1.0 + jnp.exp(chosen[0] - chosen[1]))
    mixed = first_gate * picked[0] + second_gate * picked[1]
    for k, out_ref in enumerate(out_refs):
        block = mixed[k * share : (k + 1) * share]
        if k * share < base_ref.shape[0]:
            block = block + base_ref[k * share : (k + 1) * share, :]
        out_ref[...] = block.astype(out_ref.dtype)


def combine(width, copies, rows, routes, places, base, terms, kinds):
    tokens = routes.shape[0]
    share = tokens // len(kinds)
    columns = rows.shape[1]

    def full(array):
        return pl.BlockSpec(array.shape, lambda i: (0,) * array.ndim)

    told = terms[0].shape[1] - width + len(kinds) * SLICE
    term = pl.BlockSpec((share, told), lambda i: (0, terms[0].shape[1] // told - 1))
    operands = [rows, routes, places, base, *terms]
    return pl.pallas_call(
        functools.partial(combine_kernel, width, copies, len(terms)),
        grid=(1,),
        in_specs=[full(a) for a in operands[:4]] + [term] * len(terms),
        out_specs=[pl.BlockSpec((share, columns), lambda i: (0, 0))] * len(kinds),
        out_shape=[jax.ShapeDtypeStruct((share, columns), kind) for kind in kinds],
        compiler_params=pltpu.CompilerParams(vmem_limit_bytes=40 * 1024 * 1024),
        cost_estimate=pl.CostEstimate(
            flops=4 * tokens * rows.shape[0] * columns,
            bytes_accessed=2 * rows.shape[0] * columns + 8 * tokens * columns,
            transcendentals=4 * tokens,
        ),
    )(*operands)


def place_kernel(scalars, *refs):
    piece_refs, out_ref = refs[:-1], refs[-1]
    tp = len(piece_refs)
    for k, ref in enumerate(piece_refs):
        lanes = pl.ds(pl.multiple_of(lax.rem(scalars[0] + k, tp) * SLICE, SLICE), SLICE)
        out_ref[:, lanes] = ref[...]


def place(first, slices, tile, cost=None):
    rows = slices[0].shape[0]
    width = SLICE * len(slices)
    return pl.pallas_call(
        place_kernel,
        grid_spec=pltpu.PrefetchScalarGridSpec(
            num_scalar_prefetch=1,
            grid=(rows // tile,),
            in_specs=[pl.BlockSpec((tile, SLICE), lambda i, s: (i, 0))] * len(slices),
            out_specs=pl.BlockSpec((tile, width), lambda i, s: (i, 0)),
        ),
        out_shape=jax.ShapeDtypeStruct((rows, width), slices[0].dtype),
        cost_estimate=cost,
    )(first.reshape(1), *slices)


def sum_kernel(*refs):
    *piece_refs, out_ref = refs
    total = piece_refs[0][...].astype(jnp.float32)
    for ref in piece_refs[1:]:
        total = total + ref[...].astype(jnp.float32)
    out_ref[...] = total.astype(out_ref.dtype)


def sum_of(pieces, tile):
    rows, columns = pieces[0].shape
    block = pl.BlockSpec((tile, columns), lambda i: (i, 0))
    return pl.pallas_call(
        sum_kernel,
        grid=(rows // tile,),
        in_specs=[block] * len(pieces),
        out_specs=block,
        out_shape=jax.ShapeDtypeStruct((rows, columns), jnp.bfloat16),
        cost_estimate=AHEAD,
    )(*pieces)


def same_kernel(*_):
    pass


def after(value, *arrivals):
    return pl.pallas_call(
        same_kernel,
        in_specs=[pl.BlockSpec(memory_space=pl.ANY)] * (1 + len(arrivals)),
        out_specs=pl.BlockSpec(memory_space=pl.ANY),
        out_shape=jax.ShapeDtypeStruct(value.shape, value.dtype),
        input_output_aliases={0: 0},
    )(value, *arrivals)


def joined_kernel(first_ref, rest_ref, out_ref):
    first = first_ref.shape[1]
    out_ref[:, :first] = first_ref[...]
    out_ref[:, first:] = rest_ref[...]


def joined(first, rest):
    rows = first.shape[0]
    return pl.pallas_call(
        joined_kernel,
        out_shape=jax.ShapeDtypeStruct((rows, first.shape[1] + rest.shape[1]), first.dtype),
    )(first, rest)


def per_device(
    hidden_in,
    cache_lengths,
    key_cache,
    value_cache,
    attn_norm,
    w_qkv,
    w_out,
    ffn_norm,
    router,
    routes,
    expert_gate,
    expert_up,
    expert_down,
):
    token_count, model_width = hidden_in.shape
    local_lanes = w_qkv.shape[2]
    local_heads = local_lanes // HEAD
    cache_len = key_cache.shape[1]
    tp = lax.axis_size("tp")
    me_tp = lax.axis_index("tp")
    req = lax.axis_size("req")
    expert_count = router.shape[1]
    copies = req // expert_count
    share = token_count // tp
    first_width = model_width - tp * SLICE

    def to_block(array, k):
        return lax.ppermute(array, "tp", [(i, (i + k) % tp) for i in range(tp)])

    def from_block(array, k):
        return lax.ppermute(array, "tp", [(i, (i - k) % tp) for i in range(tp)])

    def exchanged(rows):
        blocks = rows.reshape(req, CAP, -1)
        blocks = lax.all_to_all(blocks, "req", split_axis=0, concat_axis=0, tiled=True)
        return blocks.reshape(req * CAP, -1)

    def to_experts(tokens):
        packed = jnp.dot(placing, tokens, preferred_element_type=jnp.float32).astype(jnp.bfloat16)
        packed = packed.reshape(expert_count, 1, CAP, -1)
        return exchanged(
            jnp.broadcast_to(packed, (expert_count, copies, CAP, packed.shape[-1]))
        )

    def from_own(array):
        twice = jnp.concatenate([array, array], axis=0)
        return lax.dynamic_slice_in_dim(twice, me_tp * share, token_count, 0)

    expert_ids = jnp.arange(expert_count, dtype=jnp.int32)
    has = jnp.any(routes[:, :, None] == expert_ids[None, None, :], axis=1)
    token_ids = jnp.arange(token_count, dtype=jnp.int32)
    earlier = (token_ids[None, :] < token_ids[:, None]).astype(jnp.bfloat16)
    rank = jnp.dot(earlier, has.astype(jnp.bfloat16), preferred_element_type=jnp.float32).astype(
        jnp.int32
    )
    slot = from_own(jnp.where(has, rank, -1))
    rolled = from_own(routes)
    named = rolled[:, :, None] == expert_ids[None, None, :]
    slots = jnp.arange(CAP, dtype=jnp.int32)
    placing = (
        (slot.T[:, None, :] == slots[None, :, None])
        .astype(jnp.bfloat16)
        .reshape(expert_count * CAP, token_count)
    )
    places = jnp.sum(jnp.where(named, slot[:, None, :], 0), axis=2) + rolled * (copies * CAP)

    length = cache_lengths[0]
    scalars = jnp.stack([length, (me_tp + 1) % tp]).astype(jnp.int32)
    positions = length + (token_ids + scalars[1] * share) % token_count
    positions = positions.astype(jnp.float32)
    half = HEAD // 2
    frequency = jnp.exp(jnp.arange(half, dtype=jnp.float32) * (-2.0 * math.log(10000.0) / HEAD))
    angles = frequency[:, None] * positions[None, :]
    cosine = jnp.cos(angles)
    sine_part = jnp.sin(angles)
    keys_t = jnp.swapaxes(key_cache[0], 0, 1)
    values_t = jnp.swapaxes(value_cache[0], 0, 1)
    w_t = jnp.swapaxes(w_qkv, 1, 2)
    group = 3 if local_heads % 3 == 0 else 1

    def whole(*shape):
        return pl.BlockSpec(shape, lambda h, s: (0,) * len(shape))

    def head_rows(n):
        return pl.BlockSpec((group * HEAD, n), lambda h, s: (h, 0))

    *sent, own_partial = pl.pallas_call(
        functools.partial(attention_kernel, share),
        grid_spec=pltpu.PrefetchScalarGridSpec(
            num_scalar_prefetch=1,
            grid=(local_heads // group,),
            in_specs=[
                whole(token_count, model_width),
                whole(model_width),
                pl.BlockSpec((3, group * HEAD, model_width), lambda h, s: (0, h, 0)),
                whole(half, token_count),
                whole(half, token_count),
                head_rows(cache_len),
                head_rows(cache_len),
                whole(local_lanes, model_width),
            ],
            out_specs=[whole(share, model_width)] * tp,
            scratch_shapes=[
                pltpu.VMEM((model_width, token_count), jnp.bfloat16),
                pltpu.VMEM((local_heads // group, token_count, group * HEAD), jnp.bfloat16),
                pltpu.VMEM((token_count, model_width), jnp.float32),
            ],
        ),
        out_shape=[jax.ShapeDtypeStruct((share, model_width), jnp.bfloat16)] * tp,
        compiler_params=pltpu.CompilerParams(vmem_limit_bytes=62 * 1024 * 1024),
        cost_estimate=pl.CostEstimate(
            flops=token_count * local_lanes * (8 * model_width + 4 * (cache_len + token_count)),
            bytes_accessed=2 * local_lanes * (4 * model_width + 2 * cache_len),
            transcendentals=token_count * (cache_len + token_count) * local_heads,
        ),
    )(
        scalars,
        hidden_in,
        attn_norm,
        w_t,
        cosine,
        sine_part,
        keys_t,
        values_t,
        w_out,
    )
    arrived = [to_block(piece, k + 1) for k, piece in enumerate(sent)]

    gain = ffn_norm.reshape(1, model_width)
    first_residual, slice_residual, slice_raw, *messages = merge(
        me_tp, [own_partial, *arrived], hidden_in, gain, jnp.swapaxes(router, 0, 1)
    )

    slice_downs = lax.optimization_barrier(
        jnp.stack(
            [
                lax.dynamic_slice_in_dim(
                    expert_down[0], first_width + (me_tp + k) % tp * SLICE, SLICE, 1
                )
                for k in range(tp)
            ]
        )
    )

    messages = [messages[0]] + [from_block(messages[k], k) for k in range(1, tp)]
    slice_rows = to_experts(slice_raw)

    gathered = jnp.concatenate([m[:, :first_width] for m in messages], axis=0)
    gathered, slice_rows = lax.optimization_barrier((gathered, slice_rows))
    slices = [slice_rows] + [from_block(slice_rows, k) for k in range(1, tp)]
    first_rows = to_experts(gathered)
    token_rows = assemble(first_rows, place(me_tp, slices, 2 * CAP, AHEAD), gain)

    gate_proj = jnp.dot(token_rows, expert_gate[0], preferred_element_type=jnp.float32)
    up_proj = jnp.dot(token_rows, expert_up[0], preferred_element_type=jnp.float32)
    activation = (jax.nn.silu(gate_proj) * up_proj).astype(jnp.bfloat16)
    activation = lax.optimization_barrier(activation)

    first_terms = jnp.dot(
        activation, expert_down[0, :, :first_width], preferred_element_type=jnp.float32
    )
    first_back = exchanged(first_terms.astype(jnp.bfloat16))
    slice_terms = jnp.einsum(
        "rh,khs->krs", activation, slice_downs, preferred_element_type=jnp.float32
    ).astype(jnp.bfloat16)
    slice_sum = sum_of(
        [slice_terms[0]] + [to_block(slice_terms[k], k) for k in range(1, tp)], 2 * CAP
    )

    slice_back = exchanged(after(slice_sum, first_back))
    kinds = [jnp.bfloat16] * tp
    first_out, *first_shares = combine(
        model_width,
        copies,
        first_back,
        rolled,
        places,
        first_residual,
        messages,
        [jnp.float32, *kinds[1:]],
    )
    first_out = sum_of(
        [first_out] + [to_block(piece, k + 1) for k, piece in enumerate(first_shares)], share
    )
    slice_outs = combine(
        model_width, copies, slice_back, rolled, places, slice_residual, messages, kinds
    )
    slice_outs = [slice_outs[0]] + [to_block(slice_outs[k], k) for k in range(1, tp)]
    slice_outs = [slice_outs[0], *slice_outs[:0:-1]]
    return joined(first_out, place(me_tp, slice_outs, share))


def solution(mesh):
    return jax.shard_map(
        per_device,
        mesh=mesh,
        in_specs=(
            P("req", None),
            P("req"),
            P("req", None, "tp"),
            P("req", None, "tp"),
            P(),
            P(None, None, "tp"),
            P("tp", None),
            P(),
            P(),
            P("req", None),
            P("req", None, "tp"),
            P("req", None, "tp"),
            P("req", "tp", None),
        ),
        out_specs=P(("req", "tp"), None),
        check_vma=False,
    )
```

```python
import functools
import math

import jax
import jax.numpy as jnp
from jax import lax
from jax.experimental import pallas as pl
from jax.experimental.pallas import tpu as pltpu
from jax.sharding import PartitionSpec as P

HEAD = 64
TOP = 2
CAP = 96
PACK = 16
KEYS = 256
SLICE = 256
MASKED = -1e30
EPSILON = 1e-05
NT = (((1,), (1,)), ((), ()))
GRANT = pltpu.CompilerParams(vmem_limit_bytes=24 * 1024 * 1024)
AHEAD = pl.CostEstimate(flops=1 << 37, bytes_accessed=1 << 20, transcendentals=0)


def normalize(inputs, scale_gain):
    mean_square = jnp.mean(inputs * inputs, axis=-1, keepdims=True)
    return inputs * lax.rsqrt(mean_square + EPSILON) * scale_gain


def rotate_rows(inputs, cosine, sine_part):
    half_dim = inputs.shape[0] // 2
    lower_half = inputs[:half_dim]
    upper_half = inputs[half_dim:]
    return jnp.concatenate(
        [
            lower_half * cosine - upper_half * sine_part,
            lower_half * sine_part + upper_half * cosine,
        ],
        axis=0,
    )


def lane_halves(chunk, join):
    half = chunk.shape[1] // 2
    return join(chunk[:, :half], chunk[:, half:])


def attend_heads(heads, chunks, score, value):
    def row_top(scores):
        top = lane_halves(scores[0], jnp.maximum)
        for chunk in scores[1:]:
            top = jnp.maximum(top, lane_halves(chunk, jnp.maximum))
        return jnp.max(top, axis=1, keepdims=True)

    outputs = []
    ahead = [score(0, c) for c in range(chunks)]
    for g in range(heads):
        now, ahead = ahead, []
        top = row_top(now)
        totals = mixed = None
        for c in range(chunks):
            if g + 1 < heads:
                ahead.append(score(g + 1, c))
            probs = jnp.exp(now[c] - top)
            part = lane_halves(probs, jnp.add)
            totals = part if totals is None else totals + part
            part = lax.dot_general(
                probs.astype(jnp.bfloat16), value(g, c), NT, preferred_element_type=jnp.float32
            )
            mixed = part if mixed is None else mixed + part
        outputs.append(mixed / jnp.sum(totals, axis=1, keepdims=True))
    return outputs


def widened(q):
    count = q.shape[1]
    ones = jnp.where(lax.broadcasted_iota(jnp.int32, (PACK, count), 0) == 0, 1.0, 0.0)
    return jnp.concatenate([q, ones], axis=0).T.astype(jnp.bfloat16)


def head_slice(g):
    return slice(g * HEAD, (g + 1) * HEAD)


def attention_kernel(
    share,
    scalars,
    hidden_ref,
    gain_ref,
    w_ref,
    cos_ref,
    sin_ref,
    kc_ref,
    vc_ref,
    wo_ref,
    *rest,
):
    *out_refs, normed, attended, total, weights_out, copied = rest
    bring = pltpu.make_async_copy(wo_ref, weights_out, copied)
    tokens, width = hidden_ref.shape
    blocks = tokens // share
    rows_here = kc_ref.shape[0]
    heads = rows_here // HEAD
    length, shift = scalars[0], scalars[1] * share

    @pl.when(pl.program_id(0) == 0)
    def _():
        bring.start()
        for k in range(0, blocks, 2):
            pair = []
            for i in range(2):
                start = pl.multiple_of(lax.rem(scalars[1] + k + i, blocks) * share, share)
                rows = hidden_ref[pl.ds(start, share), :].astype(jnp.float32)
                pair.append(normalize(rows, gain_ref[...]))
            normed[:, k * share : (k + 2) * share] = jnp.concatenate(pair, axis=0).T.astype(
                jnp.bfloat16
            )

    weights = w_ref[...].reshape(3 * rows_here, width)
    projected = jnp.dot(weights, normed[...], preferred_element_type=jnp.float32)
    cosine, sine_part = cos_ref[...], sin_ref[...]

    cache_len = kc_ref.shape[1]
    cached = cache_len // KEYS
    pad = jnp.zeros((PACK, tokens), jnp.bfloat16)
    queries, keys, values = [], [], []
    for g in range(heads):
        q = rotate_rows(projected[head_slice(g)], cosine, sine_part).astype(jnp.bfloat16)
        queries.append(widened(q.astype(jnp.float32) * HEAD**-0.5))
        kf = rotate_rows(projected[head_slice(heads + g)], cosine, sine_part).astype(jnp.bfloat16)
        keys.append(jnp.concatenate([kf, pad], axis=0))
        values.append(projected[head_slice(2 * heads + g)].astype(jnp.bfloat16))
    slots = lax.broadcasted_iota(jnp.int32, (PACK, KEYS), 1)
    top_row = lax.broadcasted_iota(jnp.int32, (PACK, KEYS), 0) == 0
    row = lax.rem(lax.broadcasted_iota(jnp.int32, (tokens, 1), 0) + shift, tokens)
    col = lax.rem(lax.broadcasted_iota(jnp.int32, (1, tokens), 1) + shift, tokens)

    def chunk_of(c):
        return slice(c * KEYS, (c + 1) * KEYS)

    def score(g, c):
        if c == cached:
            scores = jnp.dot(queries[g], keys[g], preferred_element_type=jnp.float32)
            return jnp.where(col <= row, scores, MASKED)
        dead = top_row & (slots + c * KEYS >= length)
        bias = jnp.where(dead, MASKED, 0.0).astype(jnp.bfloat16)
        kc = jnp.concatenate([kc_ref[head_slice(g), chunk_of(c)], bias], axis=0)
        return jnp.dot(queries[g], kc, preferred_element_type=jnp.float32)

    def value(g, c):
        return values[g] if c == cached else vc_ref[head_slice(g), chunk_of(c)]

    outputs = attend_heads(heads, cached + 1, score, value)
    attended[pl.program_id(0)] = jnp.concatenate(outputs, axis=1).astype(jnp.bfloat16)

    @pl.when(pl.program_id(0) == pl.num_programs(0) - 1)
    def _():
        bring.wait()
        steps = attended.shape[0]
        total[...] = sum(
            jnp.dot(
                attended[i],
                weights_out[i * rows_here : (i + 1) * rows_here, :],
                preferred_element_type=jnp.float32,
            )
            for i in range(steps)
        )
        for i, out_ref in enumerate(out_refs):
            ahead = (i + 1) % blocks
            first = width - blocks * SLICE
            place = lax.rem(scalars[1] + i, blocks) * SLICE + first
            lanes = pl.ds(pl.multiple_of(place, SLICE), SLICE)
            out_ref[:, :first] = total[i * share : (i + 1) * share, :first].astype(out_ref.dtype)
            for j in range(blocks):
                start = (ahead + j - 1) % blocks * share
                out_ref[:, first + j * SLICE : first + (j + 1) * SLICE] = total[
                    start : start + share, lanes
                ].astype(out_ref.dtype)


def merge_kernel(share, pieces, scalars, *refs):
    piece_refs = refs[:pieces]
    hidden_ref, gain_ref, router_ref = refs[pieces : pieces + 3]
    first_ref, slice_ref, slice_raw_ref, *message_refs = refs[pieces + 3 :]
    tp = len(message_refs)
    me = scalars[0]
    first = first_ref.shape[1]
    exact = functools.partial(
        lax.dot_general,
        dimension_numbers=NT,
        precision=lax.Precision.HIGHEST,
        preferred_element_type=jnp.float32,
    )

    def terms_of(rows, lanes):
        weights = router_ref[:, lanes].astype(jnp.float32) * gain_ref[:, lanes]
        return exact(weights, rows), exact(jnp.ones_like(weights), rows * rows)

    def in_parts(logits, squares):
        row = lax.broadcasted_iota(jnp.int32, squares.shape, 0)
        last = jnp.zeros_like(squares)
        parts = []
        for p in range(3):
            part = logits.astype(jnp.bfloat16).astype(jnp.float32)
            logits = logits - part
            parts.append(part)
            part = squares.astype(jnp.bfloat16).astype(jnp.float32)
            squares = squares - part
            last = jnp.where(row == p, part, last)
        return jnp.concatenate([*parts, last], axis=0)

    def block_start(j):
        return pl.multiple_of(lax.rem(me + j, tp) * share, share)

    total = piece_refs[0][...].astype(jnp.float32)
    for ref in piece_refs[1:]:
        total = total + ref[...].astype(jnp.float32)
    own = hidden_ref[pl.ds(block_start(0), share), :first].astype(jnp.float32) + total[:, :first]
    first_ref[...] = own
    lanes = pl.ds(pl.multiple_of(first + me * SLICE, SLICE), SLICE)
    terms = []
    for j in range(tp):
        rows = hidden_ref[pl.ds(block_start(j), share), lanes].astype(jnp.float32)
        rows = rows + total[:, first + j * SLICE : first + (j + 1) * SLICE]
        slice_ref[j * share : (j + 1) * share, :] = rows
        slice_raw_ref[j * share : (j + 1) * share, :] = rows.astype(jnp.bfloat16)
        terms.append(terms_of(rows, lanes))
    terms[0] = [a + b for a, b in zip(terms[0], terms_of(own, slice(0, first)))]
    terms = [in_parts(*t) for t in terms]
    for k, message_ref in enumerate(message_refs):
        message_ref[:, :first] = own.astype(jnp.bfloat16)
        told = jnp.concatenate([terms[(j - k) % tp] for j in range(tp)], axis=0)
        message_ref[:, first:] = told.T.astype(jnp.bfloat16)


def merge(me_tp, pieces, hidden_in, gain, router_t):
    share, width = pieces[0].shape
    tp = len(pieces)
    tokens = hidden_in.shape[0]
    first = width - tp * SLICE
    length = first + tp * 4 * router_t.shape[0]
    return pl.pallas_call(
        functools.partial(merge_kernel, share, tp),
        grid_spec=pltpu.PrefetchScalarGridSpec(
            num_scalar_prefetch=1,
            grid=(1,),
            in_specs=[pl.BlockSpec(p.shape, lambda i, s: (0, 0)) for p in pieces]
            + [pl.BlockSpec(a.shape, lambda i, s: (0, 0)) for a in (hidden_in, gain, router_t)],
            out_specs=[
                pl.BlockSpec((share, first), lambda i, s: (0, 0)),
                pl.BlockSpec((tokens, SLICE), lambda i, s: (0, 0)),
                pl.BlockSpec((tokens, SLICE), lambda i, s: (0, 0)),
            ]
            + [pl.BlockSpec((share, length), lambda i, s: (0, 0))] * tp,
        ),
        out_shape=[
            jax.ShapeDtypeStruct((share, first), jnp.float32),
            jax.ShapeDtypeStruct((tokens, SLICE), jnp.float32),
            jax.ShapeDtypeStruct((tokens, SLICE), jnp.bfloat16),
        ]
        + [jax.ShapeDtypeStruct((share, length), jnp.bfloat16)] * tp,
        compiler_params=GRANT,
        cost_estimate=pl.CostEstimate(
            flops=8 * tp * share * width,
            bytes_accessed=2 * tokens * width + 4 * share * width * tp,
            transcendentals=0,
        ),
    )(me_tp.reshape(1), *pieces, hidden_in, gain, router_t)


def assemble_kernel(slices, scalars, first_ref, *refs):
    slice_refs = refs[:slices]
    gain_ref, out_ref = refs[slices:]
    first = first_ref.shape[1]
    width = out_ref.shape[1]
    rows = first_ref[...].astype(jnp.float32)
    parts = [ref[...].astype(jnp.float32) for ref in slice_refs]
    squares = jnp.sum(rows * rows, axis=1, keepdims=True)
    for part in parts:
        squares = squares + jnp.sum(part * part, axis=1, keepdims=True)
    scale = lax.rsqrt(squares / width + EPSILON)
    out_ref[:, :first] = (rows * scale * gain_ref[:, :first]).astype(jnp.bfloat16)
    for k, part in enumerate(parts):
        place = lax.rem(scalars[0] + k, slices) * SLICE + first
        lanes = pl.ds(pl.multiple_of(place, SLICE), SLICE)
        out_ref[:, lanes] = (part * scale * gain_ref[:, lanes]).astype(jnp.bfloat16)


def assemble(me_tp, first_rows, slices, gain):
    rows, first = first_rows.shape
    width = first + SLICE * len(slices)
    tile = 2 * CAP

    def tiles(n):
        return pl.BlockSpec((tile, n), lambda i, s: (i, 0))

    return pl.pallas_call(
        functools.partial(assemble_kernel, len(slices)),
        grid_spec=pltpu.PrefetchScalarGridSpec(
            num_scalar_prefetch=1,
            grid=(rows // tile,),
            in_specs=[tiles(first)]
            + [tiles(SLICE)] * len(slices)
            + [pl.BlockSpec((1, width), lambda i, s: (0, 0))],
            out_specs=tiles(width),
        ),
        out_shape=jax.ShapeDtypeStruct((rows, width), jnp.bfloat16),
        compiler_params=GRANT,
        cost_estimate=pl.CostEstimate(
            flops=8 * rows * width, bytes_accessed=4 * rows * width, transcendentals=rows
        ),
    )(me_tp.reshape(1), first_rows, *slices, gain)


def combine_kernel(width, copies, terms, rows_ref, routes_ref, places_ref, base_ref, *refs):
    term_refs, out_refs = refs[:terms], refs[terms:]
    tp = len(out_refs)
    total = term_refs[0][...].astype(jnp.float32)
    for ref in term_refs[1:]:
        total = total + ref[...].astype(jnp.float32)
    share = total.shape[0]
    tokens = tp * share
    experts = total.shape[1] // (4 * tp)
    logits = []
    for j in range(tp):
        start = 4 * experts * j
        group = [total[:, start + p * experts : start + (p + 1) * experts] for p in range(4)]
        squares = group[3][:, 0:1] + group[3][:, 1:2] + group[3][:, 2:3]
        logits.append((group[0] + group[1] + group[2]) * lax.rsqrt(squares / width + EPSILON))
    logits = jnp.concatenate(logits, axis=0)
    ids = lax.broadcasted_iota(jnp.int32, (tokens, experts), 1)
    slots = lax.broadcasted_iota(jnp.int32, (tokens, rows_ref.shape[0]), 1)
    rows = rows_ref[...]
    chosen, picked = [], []
    for k in range(TOP):
        match = routes_ref[:, k : k + 1] == ids
        chosen.append(jnp.sum(jnp.where(match, logits, 0.0), axis=1, keepdims=True))
        place = places_ref[:, k : k + 1]
        hit = slots == place
        for c in range(1, copies):
            hit = hit | (slots == place + c * CAP)
        picked.append(
            jnp.dot(
                jnp.where(hit, 1.0, 0.0).astype(jnp.bfloat16),
                rows,
                preferred_element_type=jnp.float32,
            )
        )
    first_gate = 1.0 / (1.0 + jnp.exp(chosen[1] - chosen[0]))
    second_gate = 1.0 / (1.0 + jnp.exp(chosen[0] - chosen[1]))
    mixed = first_gate * picked[0] + second_gate * picked[1]
    for k, out_ref in enumerate(out_refs):
        block = mixed[k * share : (k + 1) * share]
        if k * share < base_ref.shape[0]:
            block = block + base_ref[k * share : (k + 1) * share, :]
        out_ref[...] = block.astype(out_ref.dtype)


def combine(width, copies, rows, routes, places, base, terms, kinds):
    tokens = routes.shape[0]
    share = tokens // len(kinds)
    columns = rows.shape[1]

    def full(array):
        return pl.BlockSpec(array.shape, lambda i: (0,) * array.ndim)

    told = terms[0].shape[1] - width + len(kinds) * SLICE
    term = pl.BlockSpec((share, told), lambda i: (0, terms[0].shape[1] // told - 1))
    operands = [rows, routes, places, base, *terms]
    return pl.pallas_call(
        functools.partial(combine_kernel, width, copies, len(terms)),
        grid=(1,),
        in_specs=[full(a) for a in operands[:4]] + [term] * len(terms),
        out_specs=[pl.BlockSpec((share, columns), lambda i: (0, 0))] * len(kinds),
        out_shape=[jax.ShapeDtypeStruct((share, columns), kind) for kind in kinds],
        compiler_params=pltpu.CompilerParams(vmem_limit_bytes=40 * 1024 * 1024),
        cost_estimate=pl.CostEstimate(
            flops=4 * tokens * rows.shape[0] * columns,
            bytes_accessed=2 * rows.shape[0] * columns + 8 * tokens * columns,
            transcendentals=4 * tokens,
        ),
    )(*operands)


def sum_kernel(*refs):
    *piece_refs, out_ref = refs
    total = piece_refs[0][...].astype(jnp.float32)
    for ref in piece_refs[1:]:
        total = total + ref[...].astype(jnp.float32)
    out_ref[...] = total.astype(out_ref.dtype)


def sum_of(pieces):
    rows, columns = pieces[0].shape
    block = pl.BlockSpec((rows, columns), lambda i: (0, 0))
    return pl.pallas_call(
        sum_kernel,
        grid=(1,),
        in_specs=[block] * len(pieces),
        out_specs=block,
        out_shape=jax.ShapeDtypeStruct((rows, columns), jnp.bfloat16),
        compiler_params=GRANT,
        cost_estimate=AHEAD,
    )(*pieces)


def same_kernel(*_):
    pass


def after(value, *arrivals, cost=None):
    return pl.pallas_call(
        same_kernel,
        in_specs=[pl.BlockSpec(memory_space=pl.ANY)] * (1 + len(arrivals)),
        out_specs=pl.BlockSpec(memory_space=pl.ANY),
        out_shape=jax.ShapeDtypeStruct(value.shape, value.dtype),
        input_output_aliases={0: 0},
        cost_estimate=cost,
    )(value, *arrivals)


def finish_kernel(terms, scalars, *refs):
    term_refs, slice_refs, out_ref = refs[:terms], refs[terms:-1], refs[-1]
    tp = len(slice_refs)
    first = out_ref.shape[1] - tp * SLICE
    total = term_refs[0][...]
    for ref in term_refs[1:]:
        total = total + ref[...].astype(jnp.float32)
    out_ref[:, :first] = total.astype(jnp.bfloat16)
    for k, ref in enumerate(slice_refs):
        place = lax.rem(scalars[0] + tp - k, tp) * SLICE + first
        out_ref[:, pl.ds(pl.multiple_of(place, SLICE), SLICE)] = ref[...]


def finish(me_tp, terms, slices):
    rows, first = terms[0].shape
    width = first + len(slices) * SLICE

    def full(array):
        return pl.BlockSpec(array.shape, lambda i, s: (0, 0))

    return pl.pallas_call(
        functools.partial(finish_kernel, len(terms)),
        grid_spec=pltpu.PrefetchScalarGridSpec(
            num_scalar_prefetch=1,
            grid=(1,),
            in_specs=[full(a) for a in [*terms, *slices]],
            out_specs=pl.BlockSpec((rows, width), lambda i, s: (0, 0)),
        ),
        out_shape=jax.ShapeDtypeStruct((rows, width), jnp.bfloat16),
        compiler_params=GRANT,
        cost_estimate=pl.CostEstimate(
            flops=4 * rows * width, bytes_accessed=10 * rows * width, transcendentals=0
        ),
    )(me_tp.reshape(1), *terms, *slices)


def per_device(
    hidden_in,
    cache_lengths,
    key_cache,
    value_cache,
    attn_norm,
    w_qkv,
    w_out,
    ffn_norm,
    router,
    routes,
    expert_gate,
    expert_up,
    expert_down,
):
    token_count, model_width = hidden_in.shape
    local_lanes = w_qkv.shape[2]
    local_heads = local_lanes // HEAD
    cache_len = key_cache.shape[1]
    tp = lax.axis_size("tp")
    me_tp = lax.axis_index("tp")
    req = lax.axis_size("req")
    expert_count = router.shape[1]
    copies = req // expert_count
    share = token_count // tp
    first_width = model_width - tp * SLICE

    def to_block(array, k):
        return lax.ppermute(array, "tp", [(i, (i + k) % tp) for i in range(tp)])

    def from_block(array, k):
        return lax.ppermute(array, "tp", [(i, (i - k) % tp) for i in range(tp)])

    def exchanged(rows):
        blocks = rows.reshape(req, CAP, -1)
        blocks = lax.all_to_all(blocks, "req", split_axis=0, concat_axis=0, tiled=True)
        return blocks.reshape(req * CAP, -1)

    def to_experts(tokens):
        packed = jnp.dot(placing, tokens, preferred_element_type=jnp.float32).astype(jnp.bfloat16)
        packed = packed.reshape(expert_count, 1, CAP, -1)
        return exchanged(
            jnp.broadcast_to(packed, (expert_count, copies, CAP, packed.shape[-1]))
        )

    def from_own(array):
        twice = jnp.concatenate([array, array], axis=0)
        return lax.dynamic_slice_in_dim(twice, me_tp * share, token_count, 0)

    expert_ids = jnp.arange(expert_count, dtype=jnp.int32)
    has = jnp.any(routes[:, :, None] == expert_ids[None, None, :], axis=1)
    token_ids = jnp.arange(token_count, dtype=jnp.int32)
    earlier = (token_ids[None, :] < token_ids[:, None]).astype(jnp.bfloat16)
    rank = jnp.dot(earlier, has.astype(jnp.bfloat16), preferred_element_type=jnp.float32).astype(
        jnp.int32
    )
    slot = from_own(jnp.where(has, rank, -1))
    rolled = from_own(routes)
    named = rolled[:, :, None] == expert_ids[None, None, :]
    slots = jnp.arange(CAP, dtype=jnp.int32)
    placing = (
        (slot.T[:, None, :] == slots[None, :, None])
        .astype(jnp.bfloat16)
        .reshape(expert_count * CAP, token_count)
    )
    places = jnp.sum(jnp.where(named, slot[:, None, :], 0), axis=2) + rolled * (copies * CAP)

    length = cache_lengths[0]
    scalars = jnp.stack([length, (me_tp + 1) % tp]).astype(jnp.int32)
    positions = length + (token_ids + scalars[1] * share) % token_count
    positions = positions.astype(jnp.float32)
    half = HEAD // 2
    frequency = jnp.exp(jnp.arange(half, dtype=jnp.float32) * (-2.0 * math.log(10000.0) / HEAD))
    angles = frequency[:, None] * positions[None, :]
    cosine = jnp.cos(angles)
    sine_part = jnp.sin(angles)
    keys_t = jnp.swapaxes(key_cache[0], 0, 1)
    values_t = jnp.swapaxes(value_cache[0], 0, 1)
    w_t = jnp.swapaxes(w_qkv, 1, 2)
    group = 3 if local_heads % 3 == 0 else 1

    def whole(*shape):
        return pl.BlockSpec(shape, lambda h, s: (0,) * len(shape))

    def head_rows(n):
        return pl.BlockSpec((group * HEAD, n), lambda h, s: (h, 0))

    *sent, own_partial = pl.pallas_call(
        functools.partial(attention_kernel, share),
        grid_spec=pltpu.PrefetchScalarGridSpec(
            num_scalar_prefetch=1,
            grid=(local_heads // group,),
            in_specs=[
                whole(token_count, model_width),
                whole(model_width),
                pl.BlockSpec((3, group * HEAD, model_width), lambda h, s: (0, h, 0)),
                whole(half, token_count),
                whole(half, token_count),
                head_rows(cache_len),
                head_rows(cache_len),
                pl.BlockSpec(memory_space=pl.ANY),
            ],
            out_specs=[whole(share, model_width)] * tp,
            scratch_shapes=[
                pltpu.VMEM((model_width, token_count), jnp.bfloat16),
                pltpu.VMEM((local_heads // group, token_count, group * HEAD), jnp.bfloat16),
                pltpu.VMEM((token_count, model_width), jnp.float32),
                pltpu.VMEM((local_lanes, model_width), jnp.bfloat16),
                pltpu.SemaphoreType.DMA,
            ],
        ),
        out_shape=[jax.ShapeDtypeStruct((share, model_width), jnp.bfloat16)] * tp,
        compiler_params=pltpu.CompilerParams(vmem_limit_bytes=62 * 1024 * 1024),
        cost_estimate=pl.CostEstimate(
            flops=token_count * local_lanes * (8 * model_width + 4 * (cache_len + token_count)),
            bytes_accessed=2 * local_lanes * (4 * model_width + 2 * cache_len),
            transcendentals=token_count * (cache_len + token_count) * local_heads,
        ),
    )(
        scalars,
        hidden_in,
        attn_norm,
        w_t,
        cosine,
        sine_part,
        keys_t,
        values_t,
        w_out,
    )
    arrived = [to_block(piece, k + 1) for k, piece in enumerate(sent)]

    gain = ffn_norm.reshape(1, model_width)
    first_residual, slice_residual, slice_raw, *messages = merge(
        me_tp, [own_partial, *arrived], hidden_in, gain, jnp.swapaxes(router, 0, 1)
    )

    slice_downs = lax.optimization_barrier(
        jnp.stack(
            [
                lax.dynamic_slice_in_dim(
                    expert_down[0], first_width + (me_tp + k) % tp * SLICE, SLICE, 1
                )
                for k in range(tp)
            ]
        )
    )

    messages = [messages[0]] + [from_block(messages[k], k) for k in range(1, tp)]
    slice_rows = to_experts(slice_raw)

    gathered = jnp.concatenate([m[:, :first_width] for m in messages], axis=0)
    gathered, slice_rows = lax.optimization_barrier((gathered, slice_rows))
    slices = [from_block(slice_rows, k) for k in range(1, tp)]
    slices = [after(slice_rows, *slices, cost=AHEAD), *slices]
    first_rows = to_experts(gathered)
    token_rows = assemble(me_tp, first_rows, slices, gain)

    gate_proj = jnp.dot(token_rows, expert_gate[0], preferred_element_type=jnp.float32)
    up_proj = jnp.dot(token_rows, expert_up[0], preferred_element_type=jnp.float32)
    activation = (jax.nn.silu(gate_proj) * up_proj).astype(jnp.bfloat16)
    activation = lax.optimization_barrier(activation)

    first_terms = jnp.dot(
        activation, expert_down[0, :, :first_width], preferred_element_type=jnp.float32
    )
    first_back = exchanged(first_terms.astype(jnp.bfloat16))
    slice_terms = jnp.einsum(
        "rh,khs->krs", activation, slice_downs, preferred_element_type=jnp.float32
    ).astype(jnp.bfloat16)
    slice_sum = sum_of(
        [slice_terms[0]] + [to_block(slice_terms[k], k) for k in range(1, tp)]
    )

    slice_back = exchanged(after(slice_sum, first_back))
    kinds = [jnp.bfloat16] * tp
    first_out, *first_shares = combine(
        model_width,
        copies,
        first_back,
        rolled,
        places,
        first_residual,
        messages,
        [jnp.float32, *kinds[1:]],
    )
    first_shares = [to_block(piece, k + 1) for k, piece in enumerate(first_shares)]
    first_out = after(first_out, *first_shares, cost=AHEAD)
    slice_outs = combine(
        model_width, copies, slice_back, rolled, places, slice_residual, messages, kinds
    )
    slice_outs = [slice_outs[0]] + [to_block(slice_outs[k], k) for k in range(1, tp)]
    return finish(me_tp, [first_out, *first_shares], slice_outs)


def solution(mesh):
    return jax.shard_map(
        per_device,
        mesh=mesh,
        in_specs=(
            P("req", None),
            P("req"),
            P("req", None, "tp"),
            P("req", None, "tp"),
            P(),
            P(None, None, "tp"),
            P("tp", None),
            P(),
            P(),
            P("req", None),
            P("req", None, "tp"),
            P("req", None, "tp"),
            P("req", "tp", None),
        ),
        out_specs=P(("req", "tp"), None),
        check_vma=False,
    )
```

```python
import functools
import math

import jax
import jax.numpy as jnp
from jax import lax
from jax.experimental import pallas as pl
from jax.experimental.pallas import tpu as pltpu
from jax.sharding import PartitionSpec as P

HEAD = 64
TOP = 2
CAP = 96
PACK = 16
KEYS = 256
SLICE = 256
MASKED = -1e30
EPSILON = 1e-05
NT = (((1,), (1,)), ((), ()))
GRANT = pltpu.CompilerParams(vmem_limit_bytes=24 * 1024 * 1024)
AHEAD = pl.CostEstimate(flops=1 << 37, bytes_accessed=1 << 20, transcendentals=0)


def normalize(inputs, scale_gain):
    mean_square = jnp.mean(inputs * inputs, axis=-1, keepdims=True)
    return inputs * lax.rsqrt(mean_square + EPSILON) * scale_gain


def rotate_rows(inputs, cosine, sine_part):
    half_dim = inputs.shape[0] // 2
    lower_half = inputs[:half_dim]
    upper_half = inputs[half_dim:]
    return jnp.concatenate(
        [
            lower_half * cosine - upper_half * sine_part,
            lower_half * sine_part + upper_half * cosine,
        ],
        axis=0,
    )


def lane_halves(chunk, join):
    half = chunk.shape[1] // 2
    return join(chunk[:, :half], chunk[:, half:])


def attend_heads(heads, chunks, score, value):
    def row_top(scores):
        top = lane_halves(scores[0], jnp.maximum)
        for chunk in scores[1:]:
            top = jnp.maximum(top, lane_halves(chunk, jnp.maximum))
        return jnp.max(top, axis=1, keepdims=True)

    outputs = []
    ahead = [score(0, c) for c in range(chunks)]
    for g in range(heads):
        now, ahead = ahead, []
        top = row_top(now)
        totals = mixed = None
        for c in range(chunks):
            if g + 1 < heads:
                ahead.append(score(g + 1, c))
            probs = jnp.exp(now[c] - top)
            part = lane_halves(probs, jnp.add)
            totals = part if totals is None else totals + part
            part = lax.dot_general(
                probs.astype(jnp.bfloat16), value(g, c), NT, preferred_element_type=jnp.float32
            )
            mixed = part if mixed is None else mixed + part
        outputs.append(mixed / jnp.sum(totals, axis=1, keepdims=True))
    return outputs


def widened(q):
    count = q.shape[1]
    ones = jnp.where(lax.broadcasted_iota(jnp.int32, (PACK, count), 0) == 0, 1.0, 0.0)
    return jnp.concatenate([q, ones], axis=0).T.astype(jnp.bfloat16)


def head_slice(g):
    return slice(g * HEAD, (g + 1) * HEAD)


def attention_kernel(
    share,
    lengths,
    places,
    hidden_ref,
    gain_ref,
    w_ref,
    cos_ref,
    sin_ref,
    kc_ref,
    vc_ref,
    wo_ref,
    *rest,
):
    *out_refs, normed, attended, total, weights_out, copied = rest
    bring = pltpu.make_async_copy(wo_ref, weights_out, copied)
    tokens, width = hidden_ref.shape
    blocks = tokens // share
    rows_here = kc_ref.shape[0]
    heads = rows_here // HEAD
    length = lengths[0]
    lead = lax.rem(places[0] + 1, blocks)
    shift = lead * share

    @pl.when(pl.program_id(0) == 0)
    def _():
        bring.start()
        for k in range(0, blocks, 2):
            pair = []
            for i in range(2):
                start = pl.multiple_of(lax.rem(lead + k + i, blocks) * share, share)
                rows = hidden_ref[pl.ds(start, share), :].astype(jnp.float32)
                pair.append(normalize(rows, gain_ref[...]))
            normed[:, k * share : (k + 2) * share] = jnp.concatenate(pair, axis=0).T.astype(
                jnp.bfloat16
            )

    weights = w_ref[...].reshape(3 * rows_here, width)
    projected = jnp.dot(weights, normed[...], preferred_element_type=jnp.float32)
    cosine, sine_part = cos_ref[...], sin_ref[...]

    cache_len = kc_ref.shape[1]
    cached = cache_len // KEYS
    pad = jnp.zeros((PACK, tokens), jnp.bfloat16)
    queries, keys, values = [], [], []
    for g in range(heads):
        q = rotate_rows(projected[head_slice(g)], cosine, sine_part).astype(jnp.bfloat16)
        queries.append(widened(q.astype(jnp.float32) * HEAD**-0.5))
        kf = rotate_rows(projected[head_slice(heads + g)], cosine, sine_part).astype(jnp.bfloat16)
        keys.append(jnp.concatenate([kf, pad], axis=0))
        values.append(projected[head_slice(2 * heads + g)].astype(jnp.bfloat16))
    slots = lax.broadcasted_iota(jnp.int32, (PACK, KEYS), 1)
    top_row = lax.broadcasted_iota(jnp.int32, (PACK, KEYS), 0) == 0
    row = lax.rem(lax.broadcasted_iota(jnp.int32, (tokens, 1), 0) + shift, tokens)
    col = lax.rem(lax.broadcasted_iota(jnp.int32, (1, tokens), 1) + shift, tokens)

    def chunk_of(c):
        return slice(c * KEYS, (c + 1) * KEYS)

    def score(g, c):
        if c == cached:
            scores = jnp.dot(queries[g], keys[g], preferred_element_type=jnp.float32)
            return jnp.where(col <= row, scores, MASKED)
        dead = top_row & (slots + c * KEYS >= length)
        bias = jnp.where(dead, MASKED, 0.0).astype(jnp.bfloat16)
        kc = jnp.concatenate([kc_ref[head_slice(g), chunk_of(c)], bias], axis=0)
        return jnp.dot(queries[g], kc, preferred_element_type=jnp.float32)

    def value(g, c):
        return values[g] if c == cached else vc_ref[head_slice(g), chunk_of(c)]

    outputs = attend_heads(heads, cached + 1, score, value)
    attended[pl.program_id(0)] = jnp.concatenate(outputs, axis=1).astype(jnp.bfloat16)

    @pl.when(pl.program_id(0) == pl.num_programs(0) - 1)
    def _():
        bring.wait()
        steps = attended.shape[0]
        total[...] = sum(
            jnp.dot(
                attended[i],
                weights_out[i * rows_here : (i + 1) * rows_here, :],
                preferred_element_type=jnp.float32,
            )
            for i in range(steps)
        )
        for i, out_ref in enumerate(out_refs):
            ahead = (i + 1) % blocks
            first = width - blocks * SLICE
            place = lax.rem(lead + i, blocks) * SLICE + first
            lanes = pl.ds(pl.multiple_of(place, SLICE), SLICE)
            out_ref[:, :first] = total[i * share : (i + 1) * share, :first].astype(out_ref.dtype)
            for j in range(blocks):
                start = (ahead + j - 1) % blocks * share
                out_ref[:, first + j * SLICE : first + (j + 1) * SLICE] = total[
                    start : start + share, lanes
                ].astype(out_ref.dtype)


def merge_kernel(share, pieces, scalars, *refs):
    piece_refs = refs[:pieces]
    hidden_ref, gain_ref, router_ref = refs[pieces : pieces + 3]
    first_ref, slice_ref, slice_raw_ref, *message_refs = refs[pieces + 3 :]
    tp = len(message_refs)
    me = scalars[0]
    first = first_ref.shape[1]
    exact = functools.partial(
        lax.dot_general,
        dimension_numbers=NT,
        precision=lax.Precision.HIGHEST,
        preferred_element_type=jnp.float32,
    )

    def terms_of(rows, lanes):
        weights = router_ref[:, lanes].astype(jnp.float32) * gain_ref[:, lanes]
        return exact(weights, rows), exact(jnp.ones_like(weights), rows * rows)

    def in_parts(logits, squares):
        row = lax.broadcasted_iota(jnp.int32, squares.shape, 0)
        last = jnp.zeros_like(squares)
        parts = []
        for p in range(3):
            part = logits.astype(jnp.bfloat16).astype(jnp.float32)
            logits = logits - part
            parts.append(part)
            part = squares.astype(jnp.bfloat16).astype(jnp.float32)
            squares = squares - part
            last = jnp.where(row == p, part, last)
        return jnp.concatenate([*parts, last], axis=0)

    def block_start(j):
        return pl.multiple_of(lax.rem(me + j, tp) * share, share)

    total = piece_refs[0][...].astype(jnp.float32)
    for ref in piece_refs[1:]:
        total = total + ref[...].astype(jnp.float32)
    own = hidden_ref[pl.ds(block_start(0), share), :first].astype(jnp.float32) + total[:, :first]
    first_ref[...] = own
    lanes = pl.ds(pl.multiple_of(first + me * SLICE, SLICE), SLICE)
    terms = []
    for j in range(tp):
        rows = hidden_ref[pl.ds(block_start(j), share), lanes].astype(jnp.float32)
        rows = rows + total[:, first + j * SLICE : first + (j + 1) * SLICE]
        slice_ref[j * share : (j + 1) * share, :] = rows
        slice_raw_ref[j * share : (j + 1) * share, :] = rows.astype(jnp.bfloat16)
        terms.append(terms_of(rows, lanes))
    terms[0] = [a + b for a, b in zip(terms[0], terms_of(own, slice(0, first)))]
    terms = [in_parts(*t) for t in terms]
    for k, message_ref in enumerate(message_refs):
        message_ref[:, :first] = own.astype(jnp.bfloat16)
        told = jnp.concatenate([terms[(j - k) % tp] for j in range(tp)], axis=0)
        message_ref[:, first:] = told.T.astype(jnp.bfloat16)


def merge(me_tp, pieces, hidden_in, gain, router_t):
    share, width = pieces[0].shape
    tp = len(pieces)
    tokens = hidden_in.shape[0]
    first = width - tp * SLICE
    length = first + tp * 4 * router_t.shape[0]
    return pl.pallas_call(
        functools.partial(merge_kernel, share, tp),
        grid_spec=pltpu.PrefetchScalarGridSpec(
            num_scalar_prefetch=1,
            grid=(1,),
            in_specs=[pl.BlockSpec(p.shape, lambda i, s: (0, 0)) for p in pieces]
            + [pl.BlockSpec(a.shape, lambda i, s: (0, 0)) for a in (hidden_in, gain, router_t)],
            out_specs=[
                pl.BlockSpec((share, first), lambda i, s: (0, 0)),
                pl.BlockSpec((tokens, SLICE), lambda i, s: (0, 0)),
                pl.BlockSpec((tokens, SLICE), lambda i, s: (0, 0)),
            ]
            + [pl.BlockSpec((share, length), lambda i, s: (0, 0))] * tp,
        ),
        out_shape=[
            jax.ShapeDtypeStruct((share, first), jnp.float32),
            jax.ShapeDtypeStruct((tokens, SLICE), jnp.float32),
            jax.ShapeDtypeStruct((tokens, SLICE), jnp.bfloat16),
        ]
        + [jax.ShapeDtypeStruct((share, length), jnp.bfloat16)] * tp,
        compiler_params=GRANT,
        cost_estimate=pl.CostEstimate(
            flops=8 * tp * share * width,
            bytes_accessed=2 * tokens * width + 4 * share * width * tp,
            transcendentals=0,
        ),
    )(me_tp.reshape(1), *pieces, hidden_in, gain, router_t)


def assemble_kernel(slices, scalars, first_ref, *refs):
    slice_refs = refs[:slices]
    gain_ref, out_ref = refs[slices:]
    first = first_ref.shape[1]
    width = out_ref.shape[1]
    rows = first_ref[...].astype(jnp.float32)
    parts = [ref[...].astype(jnp.float32) for ref in slice_refs]
    squares = jnp.sum(rows * rows, axis=1, keepdims=True)
    for part in parts:
        squares = squares + jnp.sum(part * part, axis=1, keepdims=True)
    scale = lax.rsqrt(squares / width + EPSILON)
    out_ref[:, :first] = (rows * scale * gain_ref[:, :first]).astype(jnp.bfloat16)
    for k, part in enumerate(parts):
        place = lax.rem(scalars[0] + k, slices) * SLICE + first
        lanes = pl.ds(pl.multiple_of(place, SLICE), SLICE)
        out_ref[:, lanes] = (part * scale * gain_ref[:, lanes]).astype(jnp.bfloat16)


def assemble(me_tp, first_rows, slices, gain):
    rows, first = first_rows.shape
    width = first + SLICE * len(slices)
    tile = 2 * CAP

    def tiles(n):
        return pl.BlockSpec((tile, n), lambda i, s: (i, 0))

    return pl.pallas_call(
        functools.partial(assemble_kernel, len(slices)),
        grid_spec=pltpu.PrefetchScalarGridSpec(
            num_scalar_prefetch=1,
            grid=(rows // tile,),
            in_specs=[tiles(first)]
            + [tiles(SLICE)] * len(slices)
            + [pl.BlockSpec((1, width), lambda i, s: (0, 0))],
            out_specs=tiles(width),
        ),
        out_shape=jax.ShapeDtypeStruct((rows, width), jnp.bfloat16),
        compiler_params=GRANT,
        cost_estimate=pl.CostEstimate(
            flops=8 * rows * width, bytes_accessed=4 * rows * width, transcendentals=rows
        ),
    )(me_tp.reshape(1), first_rows, *slices, gain)


def combine_kernel(width, copies, terms, rows_ref, routes_ref, places_ref, base_ref, *refs):
    term_refs, out_refs = refs[:terms], refs[terms:]
    tp = len(out_refs)
    total = term_refs[0][...].astype(jnp.float32)
    for ref in term_refs[1:]:
        total = total + ref[...].astype(jnp.float32)
    share = total.shape[0]
    tokens = tp * share
    experts = total.shape[1] // (4 * tp)
    logits = []
    for j in range(tp):
        start = 4 * experts * j
        group = [total[:, start + p * experts : start + (p + 1) * experts] for p in range(4)]
        squares = group[3][:, 0:1] + group[3][:, 1:2] + group[3][:, 2:3]
        logits.append((group[0] + group[1] + group[2]) * lax.rsqrt(squares / width + EPSILON))
    logits = jnp.concatenate(logits, axis=0)
    ids = lax.broadcasted_iota(jnp.int32, (tokens, experts), 1)
    slots = lax.broadcasted_iota(jnp.int32, (tokens, rows_ref.shape[0]), 1)
    rows = rows_ref[...]
    chosen, picked = [], []
    for k in range(TOP):
        match = routes_ref[:, k : k + 1] == ids
        chosen.append(jnp.sum(jnp.where(match, logits, 0.0), axis=1, keepdims=True))
        place = places_ref[:, k : k + 1]
        hit = slots == place
        for c in range(1, copies):
            hit = hit | (slots == place + c * CAP)
        picked.append(
            jnp.dot(
                jnp.where(hit, 1.0, 0.0).astype(jnp.bfloat16),
                rows,
                preferred_element_type=jnp.float32,
            )
        )
    first_gate = 1.0 / (1.0 + jnp.exp(chosen[1] - chosen[0]))
    second_gate = 1.0 / (1.0 + jnp.exp(chosen[0] - chosen[1]))
    mixed = first_gate * picked[0] + second_gate * picked[1]
    for k, out_ref in enumerate(out_refs):
        block = mixed[k * share : (k + 1) * share]
        if k * share < base_ref.shape[0]:
            block = block + base_ref[k * share : (k + 1) * share, :]
        out_ref[...] = block.astype(out_ref.dtype)


def combine(width, copies, rows, routes, places, base, terms, kinds):
    tokens = routes.shape[0]
    share = tokens // len(kinds)
    columns = rows.shape[1]

    def full(array):
        return pl.BlockSpec(array.shape, lambda i: (0,) * array.ndim)

    told = terms[0].shape[1] - width + len(kinds) * SLICE
    term = pl.BlockSpec((share, told), lambda i: (0, terms[0].shape[1] // told - 1))
    operands = [rows, routes, places, base, *terms]
    return pl.pallas_call(
        functools.partial(combine_kernel, width, copies, len(terms)),
        grid=(1,),
        in_specs=[full(a) for a in operands[:4]] + [term] * len(terms),
        out_specs=[pl.BlockSpec((share, columns), lambda i: (0, 0))] * len(kinds),
        out_shape=[jax.ShapeDtypeStruct((share, columns), kind) for kind in kinds],
        compiler_params=pltpu.CompilerParams(vmem_limit_bytes=40 * 1024 * 1024),
        cost_estimate=pl.CostEstimate(
            flops=4 * tokens * rows.shape[0] * columns,
            bytes_accessed=2 * rows.shape[0] * columns + 8 * tokens * columns,
            transcendentals=4 * tokens,
        ),
    )(*operands)


def sum_kernel(*refs):
    *piece_refs, out_ref = refs
    total = piece_refs[0][...].astype(jnp.float32)
    for ref in piece_refs[1:]:
        total = total + ref[...].astype(jnp.float32)
    out_ref[...] = total.astype(out_ref.dtype)


def sum_of(pieces):
    rows, columns = pieces[0].shape
    block = pl.BlockSpec((rows, columns), lambda i: (0, 0))
    return pl.pallas_call(
        sum_kernel,
        grid=(1,),
        in_specs=[block] * len(pieces),
        out_specs=block,
        out_shape=jax.ShapeDtypeStruct((rows, columns), jnp.bfloat16),
        compiler_params=GRANT,
        cost_estimate=AHEAD,
    )(*pieces)


def same_kernel(*_):
    pass


def after(value, *arrivals, cost=None):
    return pl.pallas_call(
        same_kernel,
        in_specs=[pl.BlockSpec(memory_space=pl.ANY)] * (1 + len(arrivals)),
        out_specs=pl.BlockSpec(memory_space=pl.ANY),
        out_shape=jax.ShapeDtypeStruct(value.shape, value.dtype),
        input_output_aliases={0: 0},
        compiler_params=pltpu.CompilerParams(vmem_limit_bytes=1024 * 1024),
        cost_estimate=cost,
    )(value, *arrivals)


def finish_kernel(terms, scalars, *refs):
    term_refs, slice_refs, out_ref = refs[:terms], refs[terms:-1], refs[-1]
    tp = len(slice_refs)
    first = out_ref.shape[1] - tp * SLICE
    total = term_refs[0][...]
    for ref in term_refs[1:]:
        total = total + ref[...].astype(jnp.float32)
    out_ref[:, :first] = total.astype(jnp.bfloat16)
    for k, ref in enumerate(slice_refs):
        place = lax.rem(scalars[0] + tp - k, tp) * SLICE + first
        out_ref[:, pl.ds(pl.multiple_of(place, SLICE), SLICE)] = ref[...]


def finish(me_tp, terms, slices):
    rows, first = terms[0].shape
    width = first + len(slices) * SLICE

    def full(array):
        return pl.BlockSpec(array.shape, lambda i, s: (0, 0))

    return pl.pallas_call(
        functools.partial(finish_kernel, len(terms)),
        grid_spec=pltpu.PrefetchScalarGridSpec(
            num_scalar_prefetch=1,
            grid=(1,),
            in_specs=[full(a) for a in [*terms, *slices]],
            out_specs=pl.BlockSpec((rows, width), lambda i, s: (0, 0)),
        ),
        out_shape=jax.ShapeDtypeStruct((rows, width), jnp.bfloat16),
        compiler_params=GRANT,
        cost_estimate=pl.CostEstimate(
            flops=4 * rows * width, bytes_accessed=10 * rows * width, transcendentals=0
        ),
    )(me_tp.reshape(1), *terms, *slices)


def per_device(
    hidden_in,
    cache_lengths,
    key_cache,
    value_cache,
    attn_norm,
    w_qkv,
    w_out,
    ffn_norm,
    router,
    routes,
    expert_gate,
    expert_up,
    expert_down,
):
    token_count, model_width = hidden_in.shape
    local_lanes = w_qkv.shape[2]
    local_heads = local_lanes // HEAD
    cache_len = key_cache.shape[1]
    tp = lax.axis_size("tp")
    me_tp = lax.axis_index("tp")
    req = lax.axis_size("req")
    expert_count = router.shape[1]
    copies = req // expert_count
    share = token_count // tp
    first_width = model_width - tp * SLICE

    def to_block(array, k):
        return lax.ppermute(array, "tp", [(i, (i + k) % tp) for i in range(tp)])

    def from_block(array, k):
        return lax.ppermute(array, "tp", [(i, (i - k) % tp) for i in range(tp)])

    def exchanged(rows):
        blocks = rows.reshape(req, CAP, -1)
        blocks = lax.all_to_all(blocks, "req", split_axis=0, concat_axis=0, tiled=True)
        return blocks.reshape(req * CAP, -1)

    def to_experts(tokens):
        packed = jnp.dot(placing, tokens, preferred_element_type=jnp.float32).astype(jnp.bfloat16)
        packed = packed.reshape(expert_count, 1, CAP, -1)
        return exchanged(
            jnp.broadcast_to(packed, (expert_count, copies, CAP, packed.shape[-1]))
        )

    def from_own(array):
        twice = jnp.concatenate([array, array], axis=0)
        return lax.dynamic_slice_in_dim(twice, me_tp * share, token_count, 0)

    expert_ids = jnp.arange(expert_count, dtype=jnp.int32)
    has = jnp.any(routes[:, :, None] == expert_ids[None, None, :], axis=1)
    token_ids = jnp.arange(token_count, dtype=jnp.int32)
    earlier = (token_ids[None, :] < token_ids[:, None]).astype(jnp.bfloat16)
    rank = jnp.dot(earlier, has.astype(jnp.bfloat16), preferred_element_type=jnp.float32).astype(
        jnp.int32
    )
    slot = from_own(jnp.where(has, rank, -1))
    rolled = from_own(routes)
    named = rolled[:, :, None] == expert_ids[None, None, :]
    slots = jnp.arange(CAP, dtype=jnp.int32)
    placing = (
        (slot.T[:, None, :] == slots[None, :, None])
        .astype(jnp.bfloat16)
        .reshape(expert_count * CAP, token_count)
    )
    places = jnp.sum(jnp.where(named, slot[:, None, :], 0), axis=2) + rolled * (copies * CAP)

    length = cache_lengths[0]
    positions = length + (token_ids + (me_tp + 1) * share) % token_count
    positions = positions.astype(jnp.float32)
    half = HEAD // 2
    frequency = jnp.exp(jnp.arange(half, dtype=jnp.float32) * (-2.0 * math.log(10000.0) / HEAD))
    angles = frequency[:, None] * positions[None, :]
    cosine = jnp.cos(angles)
    sine_part = jnp.sin(angles)
    keys_t = jnp.swapaxes(key_cache[0], 0, 1)
    values_t = jnp.swapaxes(value_cache[0], 0, 1)
    w_t = jnp.swapaxes(w_qkv, 1, 2)
    group = 3 if local_heads % 3 == 0 else 1

    def whole(*shape):
        return pl.BlockSpec(shape, lambda h, *_: (0,) * len(shape))

    def head_rows(n):
        return pl.BlockSpec((group * HEAD, n), lambda h, *_: (h, 0))

    *sent, own_partial = pl.pallas_call(
        functools.partial(attention_kernel, share),
        grid_spec=pltpu.PrefetchScalarGridSpec(
            num_scalar_prefetch=2,
            grid=(local_heads // group,),
            in_specs=[
                whole(token_count, model_width),
                whole(model_width),
                pl.BlockSpec((3, group * HEAD, model_width), lambda h, *_: (0, h, 0)),
                whole(half, token_count),
                whole(half, token_count),
                head_rows(cache_len),
                head_rows(cache_len),
                pl.BlockSpec(memory_space=pl.ANY),
            ],
            out_specs=[whole(share, model_width)] * tp,
            scratch_shapes=[
                pltpu.VMEM((model_width, token_count), jnp.bfloat16),
                pltpu.VMEM((local_heads // group, token_count, group * HEAD), jnp.bfloat16),
                pltpu.VMEM((token_count, model_width), jnp.float32),
                pltpu.VMEM((local_lanes, model_width), jnp.bfloat16),
                pltpu.SemaphoreType.DMA,
            ],
        ),
        out_shape=[jax.ShapeDtypeStruct((share, model_width), jnp.bfloat16)] * tp,
        compiler_params=pltpu.CompilerParams(vmem_limit_bytes=62 * 1024 * 1024),
        cost_estimate=pl.CostEstimate(
            flops=token_count * local_lanes * (8 * model_width + 4 * (cache_len + token_count)),
            bytes_accessed=2 * local_lanes * (4 * model_width + 2 * cache_len),
            transcendentals=token_count * (cache_len + token_count) * local_heads,
        ),
    )(
        cache_lengths,
        me_tp.reshape(1),
        hidden_in,
        attn_norm,
        w_t,
        cosine,
        sine_part,
        keys_t,
        values_t,
        w_out,
    )
    arrived = [to_block(piece, k + 1) for k, piece in enumerate(sent)]

    gain = ffn_norm.reshape(1, model_width)
    first_residual, slice_residual, slice_raw, *messages = merge(
        me_tp, [own_partial, *arrived], hidden_in, gain, jnp.swapaxes(router, 0, 1)
    )

    slice_downs = lax.optimization_barrier(
        jnp.stack(
            [
                lax.dynamic_slice_in_dim(
                    expert_down[0], first_width + (me_tp + k) % tp * SLICE, SLICE, 1
                )
                for k in range(tp)
            ]
        )
    )

    messages = [messages[0]] + [from_block(messages[k], k) for k in range(1, tp)]
    slice_rows = to_experts(slice_raw)

    gathered = jnp.concatenate([m[:, :first_width] for m in messages], axis=0)
    gathered, slice_rows = lax.optimization_barrier((gathered, slice_rows))
    slices = [from_block(slice_rows, k) for k in range(1, tp)]
    slices = [after(slice_rows, *slices, cost=AHEAD), *slices]
    first_rows = to_experts(gathered)
    token_rows = assemble(me_tp, first_rows, slices, gain)

    gate_proj = jnp.dot(token_rows, expert_gate[0], preferred_element_type=jnp.float32)
    up_proj = jnp.dot(token_rows, expert_up[0], preferred_element_type=jnp.float32)
    activation = (jax.nn.silu(gate_proj) * up_proj).astype(jnp.bfloat16)
    activation = lax.optimization_barrier(activation)

    first_terms = jnp.dot(
        activation, expert_down[0, :, :first_width], preferred_element_type=jnp.float32
    )
    first_back = exchanged(first_terms.astype(jnp.bfloat16))
    slice_terms = jnp.einsum(
        "rh,khs->krs", activation, slice_downs, preferred_element_type=jnp.float32
    ).astype(jnp.bfloat16)
    slice_sum = sum_of(
        [slice_terms[0]] + [to_block(slice_terms[k], k) for k in range(1, tp)]
    )

    kinds = [jnp.bfloat16] * tp
    first_out, *first_shares = combine(
        model_width,
        copies,
        first_back,
        rolled,
        places,
        first_residual,
        messages,
        [jnp.float32, *kinds[1:]],
    )
    slice_back = exchanged(after(slice_sum, first_shares[-1]))
    first_shares = [to_block(piece, k + 1) for k, piece in enumerate(first_shares)]
    first_out = after(first_out, *first_shares, cost=AHEAD)
    slice_outs = combine(
        model_width, copies, slice_back, rolled, places, slice_residual, messages, kinds
    )
    slice_outs = [slice_outs[0]] + [to_block(slice_outs[k], k) for k in range(1, tp)]
    return finish(me_tp, [first_out, *first_shares], slice_outs)


def solution(mesh):
    return jax.shard_map(
        per_device,
        mesh=mesh,
        in_specs=(
            P("req", None),
            P("req"),
            P("req", None, "tp"),
            P("req", None, "tp"),
            P(),
            P(None, None, "tp"),
            P("tp", None),
            P(),
            P(),
            P("req", None),
            P("req", None, "tp"),
            P("req", None, "tp"),
            P("req", "tp", None),
        ),
        out_specs=P(("req", "tp"), None),
        check_vma=False,
    )
```

```python
import functools
import math

import jax
import jax.numpy as jnp
from jax import lax
from jax.experimental import pallas as pl
from jax.experimental.pallas import tpu as pltpu
from jax.sharding import PartitionSpec as P

HEAD = 64
TOP = 2
CAP = 96
PACK = 16
KEYS = 256
SLICE = 256
MASKED = -1e30
EPSILON = 1e-05
NT = (((1,), (1,)), ((), ()))
GRANT = pltpu.CompilerParams(vmem_limit_bytes=24 * 1024 * 1024)
AHEAD = pl.CostEstimate(flops=1 << 37, bytes_accessed=1 << 20, transcendentals=0)


def normalize(inputs, scale_gain):
    mean_square = jnp.mean(inputs * inputs, axis=-1, keepdims=True)
    return inputs * lax.rsqrt(mean_square + EPSILON) * scale_gain


def rotate_rows(inputs, cosine, sine_part):
    half_dim = inputs.shape[0] // 2
    lower_half = inputs[:half_dim]
    upper_half = inputs[half_dim:]
    return jnp.concatenate(
        [
            lower_half * cosine - upper_half * sine_part,
            lower_half * sine_part + upper_half * cosine,
        ],
        axis=0,
    )


def lane_halves(chunk, join):
    half = chunk.shape[1] // 2
    return join(chunk[:, :half], chunk[:, half:])


def attend_heads(heads, chunks, score, value):
    def row_top(scores):
        top = lane_halves(scores[0], jnp.maximum)
        for chunk in scores[1:]:
            top = jnp.maximum(top, lane_halves(chunk, jnp.maximum))
        return jnp.max(top, axis=1, keepdims=True)

    outputs = []
    ahead = [score(0, c) for c in range(chunks)]
    for g in range(heads):
        now, ahead = ahead, []
        top = row_top(now)
        mixed = None
        for c in range(chunks):
            if g + 1 < heads:
                ahead.append(score(g + 1, c))
            probs = jnp.exp(now[c] - top)
            part = lax.dot_general(
                probs.astype(jnp.bfloat16), value(g, c), NT, preferred_element_type=jnp.float32
            )
            mixed = part if mixed is None else mixed + part
        outputs.append(mixed[:, :HEAD] / mixed[:, HEAD : HEAD + 1])
    return outputs


def widened(q):
    count = q.shape[1]
    ones = jnp.where(lax.broadcasted_iota(jnp.int32, (PACK, count), 0) == 0, 1.0, 0.0)
    return jnp.concatenate([q, ones], axis=0).T.astype(jnp.bfloat16)


def head_slice(g):
    return slice(g * HEAD, (g + 1) * HEAD)


def attention_kernel(
    share,
    lengths,
    places,
    hidden_ref,
    gain_ref,
    w_ref,
    cos_ref,
    sin_ref,
    kc_ref,
    vc_ref,
    wo_ref,
    *rest,
):
    *out_refs, normed, attended, total, weights_out, copied = rest
    bring = pltpu.make_async_copy(wo_ref, weights_out, copied)
    tokens, width = hidden_ref.shape
    blocks = tokens // share
    rows_here = kc_ref.shape[0]
    heads = rows_here // HEAD
    length = lengths[0]
    lead = lax.rem(places[0] + 1, blocks)
    shift = lead * share

    @pl.when(pl.program_id(0) == 0)
    def _():
        bring.start()
        for k in range(0, blocks, 2):
            pair = []
            for i in range(2):
                start = pl.multiple_of(lax.rem(lead + k + i, blocks) * share, share)
                rows = hidden_ref[pl.ds(start, share), :].astype(jnp.float32)
                pair.append(normalize(rows, gain_ref[...]))
            normed[:, k * share : (k + 2) * share] = jnp.concatenate(pair, axis=0).T.astype(
                jnp.bfloat16
            )

    weights = w_ref[...].reshape(3 * rows_here, width)
    projected = jnp.dot(weights, normed[...], preferred_element_type=jnp.float32)
    cosine, sine_part = cos_ref[...], sin_ref[...]

    cache_len = kc_ref.shape[1]
    cached = cache_len // KEYS
    pad = jnp.zeros((PACK, tokens), jnp.bfloat16)
    queries, keys, values = [], [], []
    for g in range(heads):
        q = rotate_rows(projected[head_slice(g)], cosine, sine_part).astype(jnp.bfloat16)
        queries.append(widened(q.astype(jnp.float32) * HEAD**-0.5))
        kf = rotate_rows(projected[head_slice(heads + g)], cosine, sine_part).astype(jnp.bfloat16)
        keys.append(jnp.concatenate([kf, pad], axis=0))
        values.append(projected[head_slice(2 * heads + g)].astype(jnp.bfloat16))
    slots = lax.broadcasted_iota(jnp.int32, (PACK, KEYS), 1)
    top_row = lax.broadcasted_iota(jnp.int32, (PACK, KEYS), 0) == 0
    row = lax.rem(lax.broadcasted_iota(jnp.int32, (tokens, 1), 0) + shift, tokens)
    col = lax.rem(lax.broadcasted_iota(jnp.int32, (1, tokens), 1) + shift, tokens)

    def chunk_of(c):
        return slice(c * KEYS, (c + 1) * KEYS)

    def score(g, c):
        if c == cached:
            scores = jnp.dot(queries[g], keys[g], preferred_element_type=jnp.float32)
            return jnp.where(col <= row, scores, MASKED)
        dead = top_row & (slots + c * KEYS >= length)
        bias = jnp.where(dead, MASKED, 0.0).astype(jnp.bfloat16)
        kc = jnp.concatenate([kc_ref[head_slice(g), chunk_of(c)], bias], axis=0)
        return jnp.dot(queries[g], kc, preferred_element_type=jnp.float32)

    ones = jnp.where(top_row, 1.0, 0.0).astype(jnp.bfloat16)

    def value(g, c):
        rows = values[g] if c == cached else vc_ref[head_slice(g), chunk_of(c)]
        return jnp.concatenate([rows, ones], axis=0)

    outputs = attend_heads(heads, cached + 1, score, value)
    attended[pl.program_id(0)] = jnp.concatenate(outputs, axis=1).astype(jnp.bfloat16)

    @pl.when(pl.program_id(0) == pl.num_programs(0) - 1)
    def _():
        bring.wait()
        steps = attended.shape[0]
        total[...] = sum(
            jnp.dot(
                attended[i],
                weights_out[i * rows_here : (i + 1) * rows_here, :],
                preferred_element_type=jnp.float32,
            )
            for i in range(steps)
        )
        for i, out_ref in enumerate(out_refs):
            ahead = (i + 1) % blocks
            first = width - blocks * SLICE
            place = lax.rem(lead + i, blocks) * SLICE + first
            lanes = pl.ds(pl.multiple_of(place, SLICE), SLICE)
            out_ref[:, :first] = total[i * share : (i + 1) * share, :first].astype(out_ref.dtype)
            for j in range(blocks):
                start = (ahead + j - 1) % blocks * share
                out_ref[:, first + j * SLICE : first + (j + 1) * SLICE] = total[
                    start : start + share, lanes
                ].astype(out_ref.dtype)


def merge_kernel(share, pieces, scalars, *refs):
    piece_refs = refs[:pieces]
    hidden_ref, gain_ref, router_ref = refs[pieces : pieces + 3]
    first_ref, slice_ref, slice_raw_ref, *message_refs = refs[pieces + 3 :]
    tp = len(message_refs)
    me = scalars[0]
    first = first_ref.shape[1]
    exact = functools.partial(
        lax.dot_general,
        dimension_numbers=NT,
        precision=lax.Precision.HIGHEST,
        preferred_element_type=jnp.float32,
    )

    def terms_of(rows, lanes):
        weights = router_ref[:, lanes].astype(jnp.float32) * gain_ref[:, lanes]
        return exact(weights, rows), exact(jnp.ones_like(weights), rows * rows)

    def in_parts(logits, squares):
        row = lax.broadcasted_iota(jnp.int32, squares.shape, 0)
        last = jnp.zeros_like(squares)
        parts = []
        for p in range(3):
            part = logits.astype(jnp.bfloat16).astype(jnp.float32)
            logits = logits - part
            parts.append(part)
            part = squares.astype(jnp.bfloat16).astype(jnp.float32)
            squares = squares - part
            last = jnp.where(row == p, part, last)
        return jnp.concatenate([*parts, last], axis=0)

    def block_start(j):
        return pl.multiple_of(lax.rem(me + j, tp) * share, share)

    total = piece_refs[0][...].astype(jnp.float32)
    for ref in piece_refs[1:]:
        total = total + ref[...].astype(jnp.float32)
    own = hidden_ref[pl.ds(block_start(0), share), :first].astype(jnp.float32) + total[:, :first]
    first_ref[...] = own
    lanes = pl.ds(pl.multiple_of(first + me * SLICE, SLICE), SLICE)
    terms = []
    for j in range(tp):
        rows = hidden_ref[pl.ds(block_start(j), share), lanes].astype(jnp.float32)
        rows = rows + total[:, first + j * SLICE : first + (j + 1) * SLICE]
        slice_ref[j * share : (j + 1) * share, :] = rows
        slice_raw_ref[j * share : (j + 1) * share, :] = rows.astype(jnp.bfloat16)
        terms.append(terms_of(rows, lanes))
    terms[0] = [a + b for a, b in zip(terms[0], terms_of(own, slice(0, first)))]
    terms = [in_parts(*t) for t in terms]
    for k, message_ref in enumerate(message_refs):
        message_ref[:, :first] = own.astype(jnp.bfloat16)
        told = jnp.concatenate([terms[(j - k) % tp] for j in range(tp)], axis=0)
        message_ref[:, first:] = told.T.astype(jnp.bfloat16)


def merge(me_tp, pieces, hidden_in, gain, router_t):
    share, width = pieces[0].shape
    tp = len(pieces)
    tokens = hidden_in.shape[0]
    first = width - tp * SLICE
    length = first + tp * 4 * router_t.shape[0]
    return pl.pallas_call(
        functools.partial(merge_kernel, share, tp),
        grid_spec=pltpu.PrefetchScalarGridSpec(
            num_scalar_prefetch=1,
            grid=(1,),
            in_specs=[pl.BlockSpec(p.shape, lambda i, s: (0, 0)) for p in pieces]
            + [pl.BlockSpec(a.shape, lambda i, s: (0, 0)) for a in (hidden_in, gain, router_t)],
            out_specs=[
                pl.BlockSpec((share, first), lambda i, s: (0, 0)),
                pl.BlockSpec((tokens, SLICE), lambda i, s: (0, 0)),
                pl.BlockSpec((tokens, SLICE), lambda i, s: (0, 0)),
            ]
            + [pl.BlockSpec((share, length), lambda i, s: (0, 0))] * tp,
        ),
        out_shape=[
            jax.ShapeDtypeStruct((share, first), jnp.float32),
            jax.ShapeDtypeStruct((tokens, SLICE), jnp.float32),
            jax.ShapeDtypeStruct((tokens, SLICE), jnp.bfloat16),
        ]
        + [jax.ShapeDtypeStruct((share, length), jnp.bfloat16)] * tp,
        compiler_params=GRANT,
        cost_estimate=pl.CostEstimate(
            flops=8 * tp * share * width,
            bytes_accessed=2 * tokens * width + 4 * share * width * tp,
            transcendentals=0,
        ),
    )(me_tp.reshape(1), *pieces, hidden_in, gain, router_t)


def assemble_kernel(slices, scalars, first_ref, *refs):
    slice_refs = refs[:slices]
    gain_ref, out_ref = refs[slices:]
    first = first_ref.shape[1]
    width = out_ref.shape[1]
    rows = first_ref[...].astype(jnp.float32)
    parts = [ref[...].astype(jnp.float32) for ref in slice_refs]
    squares = jnp.sum(rows * rows, axis=1, keepdims=True)
    for part in parts:
        squares = squares + jnp.sum(part * part, axis=1, keepdims=True)
    scale = lax.rsqrt(squares / width + EPSILON)
    out_ref[:, :first] = (rows * scale * gain_ref[:, :first]).astype(jnp.bfloat16)
    for k, part in enumerate(parts):
        place = lax.rem(scalars[0] + k, slices) * SLICE + first
        lanes = pl.ds(pl.multiple_of(place, SLICE), SLICE)
        out_ref[:, lanes] = (part * scale * gain_ref[:, lanes]).astype(jnp.bfloat16)


def assemble(me_tp, first_rows, slices, gain):
    rows, first = first_rows.shape
    width = first + SLICE * len(slices)
    tile = 2 * CAP

    def tiles(n):
        return pl.BlockSpec((tile, n), lambda i, s: (i, 0))

    return pl.pallas_call(
        functools.partial(assemble_kernel, len(slices)),
        grid_spec=pltpu.PrefetchScalarGridSpec(
            num_scalar_prefetch=1,
            grid=(rows // tile,),
            in_specs=[tiles(first)]
            + [tiles(SLICE)] * len(slices)
            + [pl.BlockSpec((1, width), lambda i, s: (0, 0))],
            out_specs=tiles(width),
        ),
        out_shape=jax.ShapeDtypeStruct((rows, width), jnp.bfloat16),
        compiler_params=GRANT,
        cost_estimate=pl.CostEstimate(
            flops=8 * rows * width, bytes_accessed=4 * rows * width, transcendentals=rows
        ),
    )(me_tp.reshape(1), first_rows, *slices, gain)


def combine_kernel(width, copies, terms, rows_ref, routes_ref, places_ref, base_ref, *refs):
    term_refs, out_refs = refs[:terms], refs[terms:]
    tp = len(out_refs)
    total = term_refs[0][...].astype(jnp.float32)
    for ref in term_refs[1:]:
        total = total + ref[...].astype(jnp.float32)
    share = total.shape[0]
    tokens = tp * share
    experts = total.shape[1] // (4 * tp)
    logits = []
    for j in range(tp):
        start = 4 * experts * j
        group = [total[:, start + p * experts : start + (p + 1) * experts] for p in range(4)]
        squares = group[3][:, 0:1] + group[3][:, 1:2] + group[3][:, 2:3]
        logits.append((group[0] + group[1] + group[2]) * lax.rsqrt(squares / width + EPSILON))
    logits = jnp.concatenate(logits, axis=0)
    ids = lax.broadcasted_iota(jnp.int32, (tokens, experts), 1)
    slots = lax.broadcasted_iota(jnp.int32, (tokens, rows_ref.shape[0]), 1)
    rows = rows_ref[...]
    chosen, picked = [], []
    for k in range(TOP):
        match = routes_ref[:, k : k + 1] == ids
        chosen.append(jnp.sum(jnp.where(match, logits, 0.0), axis=1, keepdims=True))
        place = places_ref[:, k : k + 1]
        hit = slots == place
        for c in range(1, copies):
            hit = hit | (slots == place + c * CAP)
        picked.append(
            jnp.dot(
                jnp.where(hit, 1.0, 0.0).astype(jnp.bfloat16),
                rows,
                preferred_element_type=jnp.float32,
            )
        )
    first_gate = 1.0 / (1.0 + jnp.exp(chosen[1] - chosen[0]))
    second_gate = 1.0 / (1.0 + jnp.exp(chosen[0] - chosen[1]))
    mixed = first_gate * picked[0] + second_gate * picked[1]
    for k, out_ref in enumerate(out_refs):
        block = mixed[k * share : (k + 1) * share]
        if k * share < base_ref.shape[0]:
            block = block + base_ref[k * share : (k + 1) * share, :]
        out_ref[...] = block.astype(out_ref.dtype)


def combine(width, copies, rows, routes, places, base, terms, kinds):
    tokens = routes.shape[0]
    share = tokens // len(kinds)
    columns = rows.shape[1]

    def full(array):
        return pl.BlockSpec(array.shape, lambda i: (0,) * array.ndim)

    told = terms[0].shape[1] - width + len(kinds) * SLICE
    term = pl.BlockSpec((share, told), lambda i: (0, terms[0].shape[1] // told - 1))
    operands = [rows, routes, places, base, *terms]
    return pl.pallas_call(
        functools.partial(combine_kernel, width, copies, len(terms)),
        grid=(1,),
        in_specs=[full(a) for a in operands[:4]] + [term] * len(terms),
        out_specs=[pl.BlockSpec((share, columns), lambda i: (0, 0))] * len(kinds),
        out_shape=[jax.ShapeDtypeStruct((share, columns), kind) for kind in kinds],
        compiler_params=pltpu.CompilerParams(vmem_limit_bytes=40 * 1024 * 1024),
        cost_estimate=pl.CostEstimate(
            flops=4 * tokens * rows.shape[0] * columns,
            bytes_accessed=2 * rows.shape[0] * columns + 8 * tokens * columns,
            transcendentals=4 * tokens,
        ),
    )(*operands)


def sum_kernel(*refs):
    *piece_refs, out_ref = refs
    total = piece_refs[0][...].astype(jnp.float32)
    for ref in piece_refs[1:]:
        total = total + ref[...].astype(jnp.float32)
    out_ref[...] = total.astype(out_ref.dtype)


def sum_of(pieces):
    rows, columns = pieces[0].shape
    block = pl.BlockSpec((rows, columns), lambda i: (0, 0))
    return pl.pallas_call(
        sum_kernel,
        grid=(1,),
        in_specs=[block] * len(pieces),
        out_specs=block,
        out_shape=jax.ShapeDtypeStruct((rows, columns), jnp.bfloat16),
        compiler_params=GRANT,
        cost_estimate=AHEAD,
    )(*pieces)


def same_kernel(*_):
    pass


def after(value, *arrivals, cost=None):
    return pl.pallas_call(
        same_kernel,
        in_specs=[pl.BlockSpec(memory_space=pl.ANY)] * (1 + len(arrivals)),
        out_specs=pl.BlockSpec(memory_space=pl.ANY),
        out_shape=jax.ShapeDtypeStruct(value.shape, value.dtype),
        input_output_aliases={0: 0},
        compiler_params=pltpu.CompilerParams(vmem_limit_bytes=1024 * 1024),
        cost_estimate=cost,
    )(value, *arrivals)


def finish_kernel(terms, scalars, *refs):
    term_refs, slice_refs, out_ref = refs[:terms], refs[terms:-1], refs[-1]
    tp = len(slice_refs)
    first = out_ref.shape[1] - tp * SLICE
    total = term_refs[0][...]
    for ref in term_refs[1:]:
        total = total + ref[...].astype(jnp.float32)
    out_ref[:, :first] = total.astype(jnp.bfloat16)
    for k, ref in enumerate(slice_refs):
        place = lax.rem(scalars[0] + tp - k, tp) * SLICE + first
        out_ref[:, pl.ds(pl.multiple_of(place, SLICE), SLICE)] = ref[...]


def finish(me_tp, terms, slices):
    rows, first = terms[0].shape
    width = first + len(slices) * SLICE

    def full(array):
        return pl.BlockSpec(array.shape, lambda i, s: (0, 0))

    return pl.pallas_call(
        functools.partial(finish_kernel, len(terms)),
        grid_spec=pltpu.PrefetchScalarGridSpec(
            num_scalar_prefetch=1,
            grid=(1,),
            in_specs=[full(a) for a in [*terms, *slices]],
            out_specs=pl.BlockSpec((rows, width), lambda i, s: (0, 0)),
        ),
        out_shape=jax.ShapeDtypeStruct((rows, width), jnp.bfloat16),
        compiler_params=GRANT,
        cost_estimate=pl.CostEstimate(
            flops=4 * rows * width, bytes_accessed=10 * rows * width, transcendentals=0
        ),
    )(me_tp.reshape(1), *terms, *slices)


def per_device(
    hidden_in,
    cache_lengths,
    key_cache,
    value_cache,
    attn_norm,
    w_qkv,
    w_out,
    ffn_norm,
    router,
    routes,
    expert_gate,
    expert_up,
    expert_down,
):
    token_count, model_width = hidden_in.shape
    local_lanes = w_qkv.shape[2]
    local_heads = local_lanes // HEAD
    cache_len = key_cache.shape[1]
    tp = lax.axis_size("tp")
    me_tp = lax.axis_index("tp")
    req = lax.axis_size("req")
    expert_count = router.shape[1]
    copies = req // expert_count
    share = token_count // tp
    first_width = model_width - tp * SLICE

    def to_block(array, k):
        return lax.ppermute(array, "tp", [(i, (i + k) % tp) for i in range(tp)])

    def from_block(array, k):
        return lax.ppermute(array, "tp", [(i, (i - k) % tp) for i in range(tp)])

    def exchanged(rows):
        blocks = rows.reshape(req, CAP, -1)
        blocks = lax.all_to_all(blocks, "req", split_axis=0, concat_axis=0, tiled=True)
        return blocks.reshape(req * CAP, -1)

    def to_experts(tokens):
        packed = jnp.dot(placing, tokens, preferred_element_type=jnp.float32).astype(jnp.bfloat16)
        packed = packed.reshape(expert_count, 1, CAP, -1)
        return exchanged(
            jnp.broadcast_to(packed, (expert_count, copies, CAP, packed.shape[-1]))
        )

    def from_own(array):
        twice = jnp.concatenate([array, array], axis=0)
        return lax.dynamic_slice_in_dim(twice, me_tp * share, token_count, 0)

    expert_ids = jnp.arange(expert_count, dtype=jnp.int32)
    has = jnp.any(routes[:, :, None] == expert_ids[None, None, :], axis=1)
    token_ids = jnp.arange(token_count, dtype=jnp.int32)
    earlier = (token_ids[None, :] < token_ids[:, None]).astype(jnp.bfloat16)
    rank = jnp.dot(earlier, has.astype(jnp.bfloat16), preferred_element_type=jnp.float32).astype(
        jnp.int32
    )
    slot = from_own(jnp.where(has, rank, -1))
    rolled = from_own(routes)
    named = rolled[:, :, None] == expert_ids[None, None, :]
    slots = jnp.arange(CAP, dtype=jnp.int32)
    placing = (
        (slot.T[:, None, :] == slots[None, :, None])
        .astype(jnp.bfloat16)
        .reshape(expert_count * CAP, token_count)
    )
    places = jnp.sum(jnp.where(named, slot[:, None, :], 0), axis=2) + rolled * (copies * CAP)

    length = cache_lengths[0]
    positions = length + (token_ids + (me_tp + 1) * share) % token_count
    positions = positions.astype(jnp.float32)
    half = HEAD // 2
    frequency = jnp.exp(jnp.arange(half, dtype=jnp.float32) * (-2.0 * math.log(10000.0) / HEAD))
    angles = frequency[:, None] * positions[None, :]
    cosine = jnp.cos(angles)
    sine_part = jnp.sin(angles)
    keys_t = jnp.swapaxes(key_cache[0], 0, 1)
    values_t = jnp.swapaxes(value_cache[0], 0, 1)
    w_t = jnp.swapaxes(w_qkv, 1, 2)
    group = 3 if local_heads % 3 == 0 else 1

    def whole(*shape):
        return pl.BlockSpec(shape, lambda h, *_: (0,) * len(shape))

    def head_rows(n):
        return pl.BlockSpec((group * HEAD, n), lambda h, *_: (h, 0))

    *sent, own_partial = pl.pallas_call(
        functools.partial(attention_kernel, share),
        grid_spec=pltpu.PrefetchScalarGridSpec(
            num_scalar_prefetch=2,
            grid=(local_heads // group,),
            in_specs=[
                whole(token_count, model_width),
                whole(model_width),
                pl.BlockSpec((3, group * HEAD, model_width), lambda h, *_: (0, h, 0)),
                whole(half, token_count),
                whole(half, token_count),
                head_rows(cache_len),
                head_rows(cache_len),
                pl.BlockSpec(memory_space=pl.ANY),
            ],
            out_specs=[whole(share, model_width)] * tp,
            scratch_shapes=[
                pltpu.VMEM((model_width, token_count), jnp.bfloat16),
                pltpu.VMEM((local_heads // group, token_count, group * HEAD), jnp.bfloat16),
                pltpu.VMEM((token_count, model_width), jnp.float32),
                pltpu.VMEM((local_lanes, model_width), jnp.bfloat16),
                pltpu.SemaphoreType.DMA,
            ],
        ),
        out_shape=[jax.ShapeDtypeStruct((share, model_width), jnp.bfloat16)] * tp,
        compiler_params=pltpu.CompilerParams(vmem_limit_bytes=62 * 1024 * 1024),
        cost_estimate=pl.CostEstimate(
            flops=token_count * local_lanes * (8 * model_width + 4 * (cache_len + token_count)),
            bytes_accessed=2 * local_lanes * (4 * model_width + 2 * cache_len),
            transcendentals=token_count * (cache_len + token_count) * local_heads,
        ),
    )(
        cache_lengths,
        me_tp.reshape(1),
        hidden_in,
        attn_norm,
        w_t,
        cosine,
        sine_part,
        keys_t,
        values_t,
        w_out,
    )
    arrived = [to_block(piece, k + 1) for k, piece in enumerate(sent)]

    gain = ffn_norm.reshape(1, model_width)
    first_residual, slice_residual, slice_raw, *messages = merge(
        me_tp, [own_partial, *arrived], hidden_in, gain, jnp.swapaxes(router, 0, 1)
    )

    slice_downs = lax.optimization_barrier(
        jnp.stack(
            [
                lax.dynamic_slice_in_dim(
                    expert_down[0], first_width + (me_tp + k) % tp * SLICE, SLICE, 1
                )
                for k in range(tp)
            ]
        )
    )

    messages = [messages[0]] + [from_block(messages[k], k) for k in range(1, tp)]
    slice_rows = to_experts(slice_raw)

    gathered = jnp.concatenate([m[:, :first_width] for m in messages], axis=0)
    gathered, slice_rows = lax.optimization_barrier((gathered, slice_rows))
    slices = [from_block(slice_rows, k) for k in range(1, tp)]
    slices = [after(slice_rows, *slices, cost=AHEAD), *slices]
    first_rows = to_experts(gathered)
    token_rows = assemble(me_tp, first_rows, slices, gain)

    gate_proj = jnp.dot(token_rows, expert_gate[0], preferred_element_type=jnp.float32)
    up_proj = jnp.dot(token_rows, expert_up[0], preferred_element_type=jnp.float32)
    activation = (jax.nn.silu(gate_proj) * up_proj).astype(jnp.bfloat16)
    activation = lax.optimization_barrier(activation)

    first_terms = jnp.dot(
        activation, expert_down[0, :, :first_width], preferred_element_type=jnp.float32
    )
    first_back = exchanged(first_terms.astype(jnp.bfloat16))
    slice_terms = jnp.einsum(
        "rh,khs->krs", activation, slice_downs, preferred_element_type=jnp.float32
    ).astype(jnp.bfloat16)
    slice_sum = sum_of(
        [slice_terms[0]] + [to_block(slice_terms[k], k) for k in range(1, tp)]
    )

    kinds = [jnp.bfloat16] * tp
    first_out, *first_shares = combine(
        model_width,
        copies,
        first_back,
        rolled,
        places,
        first_residual,
        messages,
        [jnp.float32, *kinds[1:]],
    )
    slice_back = exchanged(after(slice_sum, first_shares[-1]))
    first_shares = [to_block(piece, k + 1) for k, piece in enumerate(first_shares)]
    first_out = after(first_out, *first_shares, cost=AHEAD)
    slice_outs = combine(
        model_width, copies, slice_back, rolled, places, slice_residual, messages, kinds
    )
    slice_outs = [slice_outs[0]] + [to_block(slice_outs[k], k) for k in range(1, tp)]
    return finish(me_tp, [first_out, *first_shares], slice_outs)


def solution(mesh):
    return jax.shard_map(
        per_device,
        mesh=mesh,
        in_specs=(
            P("req", None),
            P("req"),
            P("req", None, "tp"),
            P("req", None, "tp"),
            P(),
            P(None, None, "tp"),
            P("tp", None),
            P(),
            P(),
            P("req", None),
            P("req", None, "tp"),
            P("req", None, "tp"),
            P("req", "tp", None),
        ),
        out_specs=P(("req", "tp"), None),
        check_vma=False,
    )
```
